256 devices in a mesh: dp: 32 (over z_lo, y, core), rows: 8 (over x, z_hi).
Axes of the slice: x: 4, y: 4, z: 8 (z_hi: 2, z_lo: 4; z = z_hi * 4 + z_lo), core: 2. Of those that a mesh axis runs over, the one named last changes fastest.
Arguments:
- act_codes: bfloat16 [32, 32, 32, 704], P('dp', 'rows'), may hold values from -6 to 6
- act_exponents: int32 [32, 32, 32, 22], P('dp', 'rows'), may hold values from -5 to 1
- grad_codes: bfloat16 [32, 32, 32, 704], P('dp', 'rows'), may hold values from -6 to 6
- grad_exponents: int32 [32, 32, 32, 22], P('dp', 'rows'), may hold values from -5 to 1
- conv_kernel: float32 [7, 7, 704], replicated, may hold values from -0.875 to 0.875
- conv_bias: float32 [704], replicated, may hold values from -3 to 3
- norm_gain: float32 [704], replicated, may hold values from 0.1 to 1.9
- norm_shift: float32 [704], replicated, may hold values from -2 to 2
- proj_in: bfloat16 [2816, 704], replicated, may hold values from -0.21875 to 0.21875
- proj_bias: float32 [2816], replicated, may hold values from -2 to 2
- response_gain: float32 [2816], replicated, may hold values from -3 to 3
- proj_out: bfloat16 [2816, 704], replicated, may hold values from -0.109375 to 0.109375
Outputs:
- input_grad: bfloat16 [32, 32, 32, 704], P('dp', 'rows')
- proj_in_grad: float32 [2816, 704], P(('dp', 'rows'))
- kernel_grad: float32 [7, 7, 704], replicated
- norm_grads: float32 [2, 704], replicated
- response_grads: float32 [2, 2816], replicated
The draws below stay inside these ranges and needn't reach their ends.
All inputs are finite; a program needn't handle non-finite values.
Results may differ from the reference program's by a relative error of at most 0.0056.
Values may be sent and summed in bfloat16 or wider, within the bound.
A program may use at most 128 MiB of HBM per device.

```python
import math
import jax
import jax.numpy as jnp
from jax import lax

CHANNELS = 704
HIDDEN_SIZE = 2816
COLUMNS = 32
HEIGHT = 32
IMAGES = 32
TOKENS_ALL = 32768


def exponent_field(key, reverse_flag):
    base_draw = jax.random.randint(key, (IMAGES, HEIGHT, COLUMNS, CHANNELS // 32), -2, 2)
    row_index = jnp.arange(HEIGHT, dtype=jnp.int32)
    position = row_index * reverse_flag + (HEIGHT - 1 - row_index) * (1 - reverse_flag)
    offset = 4 * position // HEIGHT
    return (base_draw - offset[None, :, None, None]).astype(jnp.int32)


def draw_act_exponents(key, part):
    key = jax.random.fold_in(key, 11)
    return exponent_field(key, 0)


def draw_grad_exponents(key, part):
    key = jax.random.fold_in(key, 23)
    return exponent_field(key, 1)


def steps_of(key, dims, pieces, least, high):
    level = 1.0
    for dim, shards_of in pieces:
        heights = jax.random.uniform(jax.random.fold_in(jax.random.fold_in(key, 6), dim), (shards_of,), jnp.float32, least / len(pieces), high / len(pieces))
        level = level * jnp.repeat(jnp.exp(heights), dims[dim] // shards_of).reshape((-1,) + (1,) * (len(dims) - 1 - dim))
    return level


def centred(key, extent, deviation, reach, split=(), kind=jnp.bfloat16):
    values = deviation * jax.random.normal(key, extent, jnp.float32)
    if split:
        values = values * steps_of(key, extent, split, -0.22, 0.18)
    return jnp.clip(values, -reach, reach).astype(kind)


def setup_inputs(seed: int = 0) -> dict:
    seeds = jax.random.split(jax.random.key(seed), 13)
    return {
        "act_codes": centred(seeds[0], (IMAGES, HEIGHT, COLUMNS, CHANNELS), 1.0, 6.0, ((0, 32), (1, 8))),
        "act_exponents": draw_act_exponents(jax.random.fold_in(seeds[12], 71), 0),
        "grad_codes": centred(seeds[2], (IMAGES, HEIGHT, COLUMNS, CHANNELS), 1.0, 6.0, ((0, 32), (1, 8))),
        "grad_exponents": draw_grad_exponents(jax.random.fold_in(seeds[12], 71), 0),
        "conv_kernel": centred(seeds[4], (7, 7, CHANNELS), 49 ** -0.5, 0.875, (), jnp.float32),
        "conv_bias": centred(seeds[5], (CHANNELS,), 0.5, 3.0, (), jnp.float32),
        "norm_gain": jnp.clip(1.0 + 0.18 * jax.random.normal(seeds[6], (CHANNELS,), jnp.float32), 0.1, 1.9),
        "norm_shift": centred(seeds[7], (CHANNELS,), 0.3, 2.0, (), jnp.float32),
        "proj_in": centred(seeds[8], (HIDDEN_SIZE, CHANNELS), CHANNELS ** -0.5, 0.21875),
        "proj_bias": centred(seeds[9], (HIDDEN_SIZE,), 0.3, 2.0, (), jnp.float32),
        "response_gain": centred(seeds[10], (HIDDEN_SIZE,), 0.5, 3.0, (), jnp.float32),
        "proj_out": centred(seeds[11], (HIDDEN_SIZE, CHANNELS), HIDDEN_SIZE ** -0.5, 0.109375),
    }


NORM_EPSILON = 1e-06
RESPONSE_EPSILON = 1e-06
HALF_ROOT = 0.7071067811865476
NORMAL_PEAK = 0.3989422804014327

def block_scaled(quantized, exponents):
    array_shape = quantized.shape
    grouped = quantized.astype(jnp.float32).reshape(array_shape[:-1] + (array_shape[-1] // 32, 32))
    scaled = grouped * jnp.exp2(exponents.astype(jnp.float32))[..., None]
    return scaled.reshape(array_shape).astype(jnp.bfloat16)

def depthwise(padded, weights, out_rows, out_columns):
    result = jnp.zeros((out_rows, out_columns, padded.shape[-1]), jnp.float32)
    for tap_row in range(7):
        for tap_column in range(7):
            window = padded[tap_row:tap_row + out_rows, tap_column:tap_column + out_columns, :].astype(jnp.float32)
            result = result + window * weights[tap_row, tap_column]
    return result

def kernel_terms(padded, upstream, out_rows, out_columns):
    tap_totals = []
    for tap_row in range(7):
        for tap_column in range(7):
            window = padded[tap_row:tap_row + out_rows, tap_column:tap_column + out_columns, :].astype(jnp.float32)
            tap_totals.append(lax.optimization_barrier(jnp.sum(window * upstream, axis=(0, 1))))
    return jnp.stack(tap_totals).reshape(7, 7, padded.shape[-1])

def reference(act_codes, act_exponents, grad_codes, grad_exponents, conv_kernel, conv_bias, norm_gain, norm_shift, proj_in, proj_bias, response_gain, proj_out):
    grad_scale = 1.0 / math.sqrt(TOKENS_ALL)
    token_count = HEIGHT * COLUMNS

    def one_image(totals, slices):
        image_codes, image_exponents, grad_image, grad_exponent_image = slices
        inputs = block_scaled(image_codes, image_exponents)
        padded_in = jnp.pad(inputs, ((3, 3), (3, 3), (0, 0)))
        mixed = depthwise(padded_in, conv_kernel, HEIGHT, COLUMNS) + conv_bias
        mixed_flat = mixed.reshape(token_count, CHANNELS)
        centered = mixed_flat - lax.optimization_barrier(jnp.mean(mixed_flat, axis=1, keepdims=True))
        inverse = lax.rsqrt(lax.optimization_barrier(jnp.mean(centered * centered, axis=1, keepdims=True)) + NORM_EPSILON)
        normed = centered * inverse
        normed_in = (normed * norm_gain + norm_shift).astype(jnp.bfloat16)
        preact = jnp.dot(normed_in, proj_in.T, preferred_element_type=jnp.float32) + proj_bias
        cumulative = 0.5 * (1.0 + lax.erf(preact * HALF_ROOT))
        activation = preact * cumulative
        squares = lax.optimization_barrier(jnp.sum(activation * activation, axis=0))
        magnitude = jnp.sqrt(squares + RESPONSE_EPSILON)
        denominator = jnp.mean(magnitude) + RESPONSE_EPSILON
        response = magnitude / denominator
        upstream = block_scaled(grad_image, grad_exponent_image).reshape(token_count, CHANNELS)
        down_grad = jnp.dot(upstream, proj_out.T, preferred_element_type=jnp.float32)
        products = lax.optimization_barrier(jnp.sum(down_grad * activation, axis=0))
        scaled_products = response_gain * products
        magnitude_grad = scaled_products / denominator - jnp.sum(scaled_products * magnitude) / (denominator * denominator * HIDDEN_SIZE)
        activation_grad = down_grad * (1.0 + response_gain * response) + activation * (magnitude_grad / magnitude)
        density = NORMAL_PEAK * jnp.exp(-0.5 * preact * preact)
        preact_grad = (activation_grad * (cumulative + preact * density)).astype(jnp.bfloat16)
        inner_term = jnp.dot(preact_grad.T, normed_in, preferred_element_type=jnp.float32)
        normed_grad = jnp.dot(preact_grad, proj_in, preferred_element_type=jnp.float32)
        gain_part = lax.optimization_barrier(jnp.sum(normed_grad * normed, axis=0))
        shift_part = lax.optimization_barrier(jnp.sum(normed_grad, axis=0))
        scaled_grad = normed_grad * norm_gain
        mixed_grad = (inverse * (scaled_grad - lax.optimization_barrier(jnp.mean(scaled_grad, axis=1, keepdims=True)) - normed * lax.optimization_barrier(jnp.mean(scaled_grad * normed, axis=1, keepdims=True)))).astype(jnp.bfloat16)
        mixed_grid = mixed_grad.reshape(HEIGHT, COLUMNS, CHANNELS)
        grad_padded = jnp.pad(mixed_grid, ((3, 3), (3, 3), (0, 0)))
        spread = depthwise(grad_padded, conv_kernel[::-1, ::-1], HEIGHT, COLUMNS)
        input_grad = (upstream.reshape(HEIGHT, COLUMNS, CHANNELS).astype(jnp.float32) + spread).astype(jnp.bfloat16)
        kernel_part = kernel_terms(padded_in, mixed_grid.astype(jnp.float32), HEIGHT, COLUMNS)
        norm_part = jnp.stack([gain_part, shift_part])
        response_part = jnp.stack([response * products, lax.optimization_barrier(jnp.sum(down_grad, axis=0))])
        updated = (totals[0] + inner_term, totals[1] + kernel_part, totals[2] + norm_part, totals[3] + response_part)
        return (updated, input_grad)
    start_totals = (jnp.zeros((HIDDEN_SIZE, CHANNELS), jnp.float32), jnp.zeros((7, 7, CHANNELS), jnp.float32), jnp.zeros((2, CHANNELS), jnp.float32), jnp.zeros((2, HIDDEN_SIZE), jnp.float32))
    summed, input_grad = lax.scan(one_image, start_totals, (act_codes, act_exponents, grad_codes, grad_exponents))
    return (input_grad, summed[0] * grad_scale, summed[1] * grad_scale, summed[2] * grad_scale, summed[3] * grad_scale)
```

```python
import math

import jax
import jax.numpy as jnp
from jax import lax
from jax.experimental import pallas as pl
from jax.experimental.pallas import tpu as pltpu
from jax.sharding import PartitionSpec as P

NORM_EPSILON = 1e-06
RESPONSE_EPSILON = 1e-06
HALF_ROOT = 0.7071067811865476
NORMAL_PEAK = 0.3989422804014327

C = 704
CP = 768
CT = CP // 128
H = 2816
HT = H // 128
R = 4
W = 32
T = R * W
S = H // 8
B = S // 4
U = B // 8
F32 = jnp.float32
BF16 = jnp.bfloat16

ALPHA = (
    0.00022905065861350646,
    0.0034082910107109506,
    0.050955695062380861,
    0.18520832239976145,
    1.128379143519084,
)
BETA = (
    -1.1791602954361697e-7,
    0.000023547966471313185,
    0.0010179625278914885,
    0.014070470171167667,
    0.11098505178285362,
    0.49746925110067538,
    1.0,
)


def erf(v):
    v = jnp.clip(v, -3.7439211627767994, 3.7439211627767994)
    s = v * v
    top = jnp.full_like(s, ALPHA[0])
    for c in ALPHA[1:]:
        top = top * s + c
    low = jnp.full_like(s, BETA[0])
    for c in BETA[1:]:
        low = low * s + c
    return v * top / low


def lanes(i, n=128):
    return pl.ds(pl.multiple_of(i * n, n), n)


def moved(v, d):
    if d == 0:
        return v
    w = lax.broadcasted_iota(jnp.int32, v.shape, 0) + d
    return jnp.where((w >= 0) & (w < W), pltpu.roll(v, (-d) % W, 0), 0.0)


def depthwise(rows, weight):
    out = [None] * R
    for b in range(7):
        for r in range(R):
            acc = rows[r] * weight(0, b)
            for a in range(1, 7):
                acc = acc + rows[r + a] * weight(a, b)
            acc = moved(acc, b - 3)
            out[r] = acc if out[r] is None else out[r] + acc
    return out


def body(
    act_ref, aexp_ref, grad_ref, gexp_ref, ck_ref, cb_ref, gain_ref, shift_ref,
    win_hbm, pb_ref, rg_ref, wout_hbm,
    ig_ref, dw_ref, kg_ref, ng_ref, rp_ref,
    win, wout, ckp, prm, sx, su, xs, up, mg, mx, normed, inv, ni, niall,
    act, gp, dg, pg, pgt, pgr, stq, stp, rq, rp, coef, dwf, dwb, xr, zacc, zs, zr,
    ngb, xf, red, redr, ysum, yr, zsum, zar, fin, og,
    wsem, bsem, ssend, srecv, hsend, hrecv, gsend, grecv, nsend, nrecv, fsend, frecv,
    psend, precv, lsem, xsend, xrecv, zsend, zrecv, rsend, rrecv, ysend, yrecv,
    asend, arecv, qsend, qrecv, osend, orecv,
):
    dp, rw = lax.axis_index("dp"), lax.axis_index("rows")
    core = lax.rem(dp, 2)
    y = lax.rem(lax.div(dp, 2), 4)
    zl = lax.div(dp, 8)
    x = lax.div(rw, 2)
    zh = lax.rem(rw, 2)
    z = zh * 4 + zl
    gx = 2 * x + core
    gy = 2 * y + core

    def dev(x=x, y=y, zl=zl, zh=zh, core=core):
        return {"dp": (zl * 4 + y) * 2 + core, "rows": x * 2 + zh}

    def in_gx(i):
        m = lax.rem(gx + i, 8)
        return dev(x=lax.div(m, 2), core=lax.rem(m, 2))

    def in_gy(i):
        m = lax.rem(gy + i, 8)
        return dev(y=lax.div(m, 2), core=lax.rem(m, 2)), m

    def in_z(i):
        m = lax.rem(z + i, 8)
        return dev(zl=lax.rem(m, 4), zh=lax.div(m, 4))

    def same(d):
        return (d["dp"] == dp) & (d["rows"] == rw)

    swap = core != zh
    swap_dev = dev(zh=1 - zh, core=1 - core)
    sib = dev(core=1 - core)

    def owner(g):
        return dev(
            x=g // 2,
            y=2 * core + lax.div(x, 2),
            zl=y,
            zh=jnp.int32(g % 2),
            core=lax.rem(x, 2),
        )

    def source(k):
        return dev(
            x=2 * lax.rem(y, 2) + core,
            y=zl,
            zl=jnp.int32(k % 4),
            zh=jnp.int32(k // 4),
            core=lax.div(y, 2),
        )

    def remote(src, dst, send, recv, to):
        return pltpu.make_async_remote_copy(
            src_ref=src, dst_ref=dst, send_sem=send, recv_sem=recv,
            device_id=to, device_id_type=pl.DeviceIdType.MESH,
        )

    win_copy = pltpu.make_async_copy(win_hbm, win.at[pl.ds(0, C)], wsem.at[0])
    wout_copy = pltpu.make_async_copy(wout_hbm, wout.at[pl.ds(0, C)], wsem.at[1])
    win_copy.start()
    wout_copy.start()

    barrier = pltpu.get_barrier_semaphore()

    def greet(d):
        pl.semaphore_signal(
            barrier, inc=1, device_id=d, device_id_type=pl.DeviceIdType.MESH
        )

    @pl.when(swap)
    def _():
        greet(swap_dev)

    for i in range(1, 8):
        greet(in_gx(i))
    for i in range(1, 8):
        d, m = in_gy(i)
        greet(d)
    for i in range(1, 8):
        greet(in_z(i))
    guests = 21 + jnp.where(swap, 1, 0)
    for g in range(8):
        for d in (owner(g), source(g)):
            other = jnp.logical_not(same(d))
            guests = guests + jnp.where(other, 1, 0)

            @pl.when(other)
            def _():
                greet(d)

    member = lax.broadcasted_iota(jnp.int32, (C // 32, CP), 1) // 32
    block = lax.broadcasted_iota(jnp.int32, (C // 32, CP), 0)
    spread = jnp.where(member == block, 1.0, 0.0).astype(BF16)

    def scaled(codes, exps, out):
        for r in range(R):
            power = jnp.exp2(exps[:, r, :].astype(F32)).astype(BF16)
            full = lax.dot_general(
                power, spread, (((0,), (0,)), ((), ())), preferred_element_type=F32
            )
            out[r, :, C - 64 : CP] = jnp.zeros((W, CP - C + 64), BF16)
            out[r, :, 0:C] = (codes[r].astype(F32) * full[:, 0:C]).astype(BF16)

    scaled(act_ref, aexp_ref, sx)

    pl.semaphore_wait(barrier, guests)

    swap_x = remote(sx, xs.at[pl.ds(3, R)], ssend.at[0], srecv.at[0], swap_dev)
    swap_u = remote(su, up, ssend.at[1], srecv.at[1], swap_dev)

    @pl.when(swap)
    def _():
        swap_x.start()

    scaled(grad_ref, gexp_ref, su)

    @pl.when(swap)
    def _():
        swap_u.start()

    @pl.when(jnp.logical_not(swap))
    def _():
        xs[3 : 3 + R] = sx[...]
        up[...] = su[...]

    ckp[...] = jnp.zeros_like(ckp)
    prm[...] = jnp.zeros_like(prm)
    ckp[:, 0:7, 0:C] = ck_ref[...]
    prm[0:1, 0:C] = cb_ref[...]
    prm[1:2, 0:C] = gain_ref[...]
    prm[2:3, 0:C] = shift_ref[...]
    win[C:CP, :] = jnp.zeros((CP - C, H), BF16)
    wout[C:CP, :] = jnp.zeros((CP - C, H), BF16)
    first, last = gx == 0, gx == 7

    @pl.when(first)
    def _():
        xs[0:3] = jnp.zeros((3, W, CP), BF16)
        mg[0:3] = jnp.zeros((3, W, CP), BF16)

    @pl.when(last)
    def _():
        xs[7:10] = jnp.zeros((3, W, CP), BF16)
        mg[7:10] = jnp.zeros((3, W, CP), BF16)

    below, above = lax.rem(gx + 1, 8), lax.rem(gx + 7, 8)
    below_dev = dev(x=lax.div(below, 2), core=lax.rem(below, 2))
    above_dev = dev(x=lax.div(above, 2), core=lax.rem(above, 2))

    def halo(buf, base):
        down = remote(buf.at[pl.ds(4, 3)], buf.at[pl.ds(0, 3)],
                      hsend.at[base], hrecv.at[base], below_dev)
        upward = remote(buf.at[pl.ds(3, 3)], buf.at[pl.ds(7, 3)],
                        hsend.at[base + 1], hrecv.at[base + 1], above_dev)

        def start():
            @pl.when(jnp.logical_not(last))
            def _():
                down.start()

            @pl.when(jnp.logical_not(first))
            def _():
                upward.start()

        def arrive():
            @pl.when(jnp.logical_not(first))
            def _():
                down.wait_recv()

            @pl.when(jnp.logical_not(last))
            def _():
                upward.wait_recv()

        def finish():
            @pl.when(jnp.logical_not(last))
            def _():
                down.wait_send()

            @pl.when(jnp.logical_not(first))
            def _():
                upward.wait_send()

        return start, arrive, finish

    @pl.when(swap)
    def _():
        swap_x.wait_recv()

    x_start, x_arrive, x_finish = halo(xs, 0)
    x_start()
    x_arrive()

    def conv_tile(t, _):
        at = lanes(t)
        rows = [xs[i, :, at].astype(F32) for i in range(R + 6)]
        out = depthwise(rows, lambda a, b: ckp[a, b : b + 1, at])
        for r in range(R):
            mx[pl.ds(r * W, W), at] = out[r] + prm[0:1, at]
        return 0

    lax.fori_loop(0, CT, conv_tile, 0)

    inside = lax.broadcasted_iota(jnp.int32, (W, CP), 1) < C

    def norm_block(r, _):
        at = pl.ds(pl.multiple_of(r * W, W), W)
        v = mx[at, :]
        centered = jnp.where(inside, v - jnp.sum(v, axis=1, keepdims=True) / C, 0.0)
        var = jnp.sum(centered * centered, axis=1, keepdims=True) / C
        inverse = lax.rsqrt(var + NORM_EPSILON)
        n = centered * inverse
        normed[at, :] = n
        inv[at, :] = jnp.broadcast_to(inverse, (W, 128))
        ni[at, :] = (n * prm[1:2, :] + prm[2:3, :]).astype(BF16)
        return 0

    lax.fori_loop(0, R, norm_block, 0)

    ni_copies = []
    for i in range(1, 4):
        to = dev(y=lax.rem(y + i, 4))
        ni_copies.append(
            remote(ni, niall.at[gy], nsend.at[i - 1], nrecv.at[i - 1], to)
        )
    for c in ni_copies:
        c.start()
    niall[gy] = ni[...]

    stq[...] = jnp.zeros_like(stq)
    stp[...] = jnp.zeros_like(stp)
    red[...] = jnp.zeros_like(red)
    win_copy.wait()

    def active(i, _):
        at = lanes(i, 256)
        p = jnp.dot(ni[...], win[:, at], preferred_element_type=F32) + pb_ref[:, at]
        phi = 0.5 * (1.0 + erf(p * HALF_ROOT))
        v = p * phi
        act[:, at] = v
        gp[:, at] = phi + p * (NORMAL_PEAK * jnp.exp(-0.5 * p * p))
        s = jnp.sum(v * v, axis=0, keepdims=True)
        stq[pl.ds(2 * i, 1), :] = s[:, 0:128]
        stq[pl.ds(2 * i + 1, 1), :] = s[:, 128:256]
        return 0

    lax.fori_loop(0, HT // 2, active, 0)

    def to_group(src, dst, send, recv):
        return [
            remote(src, dst.at[gx], send.at[i - 1], recv.at[i - 1], in_gx(i))
            for i in range(1, 8)
        ]

    q_copies = to_group(stq, rq, gsend.at[0], grecv.at[0])
    for c in q_copies:
        c.start()
    rq[gx] = stq[...]

    @pl.when(swap)
    def _():
        swap_u.wait_recv()

    wout_copy.wait()
    uf = up[...].reshape(T, CP)

    def downward(i, _):
        at = lanes(i, 256)
        d = jnp.dot(uf, wout[:, at], preferred_element_type=F32)
        dg[:, at] = d
        s = jnp.sum(d * act[:, at], axis=0, keepdims=True)
        stp[pl.ds(2 * i, 1), :] = s[:, 0:128]
        stp[pl.ds(2 * i + 1, 1), :] = s[:, 128:256]
        e = jnp.sum(d, axis=0, keepdims=True)
        red[pl.ds(360 + 2 * i, 1), :] = e[:, 0:128]
        red[pl.ds(361 + 2 * i, 1), :] = e[:, 128:256]
        return 0

    lax.fori_loop(0, HT // 2, downward, 0)
    p_copies = to_group(stp, rp, gsend.at[1], grecv.at[1])
    for c in p_copies:
        c.start()
    rp[gx] = stp[...]

    for c in q_copies:
        c.wait_recv()
    squares = rq[0, 0:HT]
    for i in range(1, 8):
        squares = squares + rq[i, 0:HT]
    magnitude = jnp.sqrt(squares + RESPONSE_EPSILON)
    denominator = jnp.sum(magnitude) / H + RESPONSE_EPSILON
    response = magnitude / denominator
    coef[0, 0:HT] = 1.0 + rg_ref[...] * response
    red[336 : 336 + HT] = response * stp[0:HT]
    for c in p_copies:
        c.wait_recv()
    products = rp[0, 0:HT]
    for i in range(1, 8):
        products = products + rp[i, 0:HT]
    scaled_products = rg_ref[...] * products
    magnitude_grad = scaled_products / denominator - jnp.sum(
        scaled_products * magnitude
    ) / (denominator * denominator * H)
    coef[1, 0:HT] = magnitude_grad / magnitude

    def preact(i, _):
        at = lanes(i)
        a = coef[0, pl.ds(i, 1), :]
        b = coef[1, pl.ds(i, 1), :]
        g = (dg[:, at] * a + act[:, at] * b) * gp[:, at]
        pg[:, at] = g.astype(BF16)
        pgt[lanes(i), :] = g.T.astype(BF16)
        return 0

    lax.fori_loop(0, HT, preact, 0)

    own = pl.ds(pl.multiple_of(gy * 128, 128), 128)
    a_copies = []
    for i in range(1, 8):
        to, m = in_gy(i)
        piece = pgt.at[pl.ds(pl.multiple_of(m * S, 32), S)]
        a_copies.append(
            remote(piece, pgr.at[:, own], psend.at[i - 1], precv.at[i - 1], to)
        )
    for c in a_copies:
        c.start()
    pgr[:, own] = pgt[pl.ds(pl.multiple_of(gy * S, 32), S), :]

    for c in ni_copies:
        c.wait_recv()
    f_copies = []
    for k in range(4):
        piece = niall.at[2 * k + core]
        f_copies.append(remote(piece, piece, fsend.at[k], frecv.at[k], sib))
    for c in f_copies:
        c.start()

    ngb[...] = lax.dot_general(
        pg[...], win[...], (((1,), (1,)), ((), ())), preferred_element_type=F32
    )

    def norm_grad(r, sums):
        at = pl.ds(pl.multiple_of(r * W, W), W)
        g = ngb[at, :]
        n = normed[at, :]
        gn = g * n
        s = g * prm[1:2, :]
        m1 = jnp.sum(s, axis=1, keepdims=True) / C
        m2 = jnp.sum(s * n, axis=1, keepdims=True) / C
        v = inv[at, :][:, 0:1] * (s - m1 - n * m2)
        mg[3 + r] = jnp.where(inside, v, 0.0).astype(BF16)
        return (
            sums[0] + jnp.sum(gn, axis=0, keepdims=True),
            sums[1] + jnp.sum(g, axis=0, keepdims=True),
        )

    zero = jnp.zeros((1, CP), F32)
    gain_part, shift_part = lax.fori_loop(0, R, norm_grad, (zero, zero))
    m_start, m_arrive, m_finish = halo(mg, 2)
    m_start()

    def kernel_tile(t, _):
        at = lanes(t)
        for i in range(R + 6):
            xf[i] = xs[i, :, at].astype(F32)
        g = [mg[3 + r, :, at].astype(F32) for r in range(R)]
        base = t * 56
        for b in range(7):
            gs = [moved(v, 3 - b) for v in g]
            for a in range(7):
                s = xf[a] * gs[0]
                for r in range(1, R):
                    s = s + xf[a + r] * gs[r]
                red[pl.ds(base + a * 8 + b, 1), :] = jnp.sum(s, axis=0, keepdims=True)
        return 0

    lax.fori_loop(0, CT, kernel_tile, 0)
    for t in range(CT):
        red[56 * t + 7 : 56 * t + 8, :] = gain_part[:, 128 * t : 128 * t + 128]
        red[56 * t + 15 : 56 * t + 16, :] = shift_part[:, 128 * t : 128 * t + 128]

    def share(m):
        return pl.ds(pl.multiple_of(m * 48, 8), 48)

    r_copies = []
    for i in range(1, 8):
        m = lax.rem(gx + i, 8)
        r_copies.append(
            remote(red.at[share(m)], redr.at[gx], rsend.at[i - 1], rrecv.at[i - 1], in_gx(i))
        )
    for c in r_copies:
        c.start()
    redr[gx] = red[share(gx), :]

    for c in a_copies:
        c.wait_recv()
    for c in f_copies:
        c.wait_recv()
    dwf[S : S + 8, :] = jnp.zeros((8, CP), F32)
    dwf[0:S, :] = jnp.dot(
        pgr[...], niall[...].reshape(8 * T, CP), preferred_element_type=F32
    )
    for k in range(4):
        dwb[k] = dwf[B * k : B * k + 96, :].astype(BF16)
    x_copies = []
    for i in range(1, 4):
        k = lax.rem(x + i, 4)
        x_copies.append(
            remote(dwb.at[k], xr.at[i - 1], xsend.at[i - 1], xrecv.at[i - 1], dev(x=k))
        )
    for c in x_copies:
        c.start()

    m_arrive()

    def back_tile(t, _):
        at = lanes(t)
        rows = [mg[i, :, at].astype(F32) for i in range(R + 6)]
        out = depthwise(rows, lambda a, b: ckp[6 - a, 6 - b : 7 - b, at])
        for r in range(R):
            sx[r, :, at] = (out[r] + up[r, :, at].astype(F32)).astype(BF16)
        return 0

    @pl.when(swap)
    def _():
        swap_x.wait_send()

    lax.fori_loop(0, CT, back_tile, 0)
    og[...] = sx[:, :, 0:C]
    o_copy = remote(og, ig_ref, osend.at[0], orecv.at[0], swap_dev)
    o_local = pltpu.make_async_copy(og, ig_ref, lsem.at[0])

    @pl.when(swap)
    def _():
        o_copy.start()

    @pl.when(jnp.logical_not(swap))
    def _():
        o_local.start()

    for c in r_copies:
        c.wait_recv()
    total = redr[0]
    for i in range(1, 8):
        total = total + redr[i]
    ysum[...] = total
    y_copies = [
        remote(ysum, yr.at[y], ysend.at[i - 1], yrecv.at[i - 1], dev(y=lax.rem(y + i, 4)))
        for i in range(1, 4)
    ]
    for c in y_copies:
        c.start()
    yr[y] = total

    for c in x_copies:
        c.wait_recv()
    zacc[...] = dwf[pl.ds(pl.multiple_of(x * B, 8), 96), :]
    zacc[...] = (
        zacc[...] + xr[0].astype(F32) + xr[1].astype(F32) + xr[2].astype(F32)
    )
    for g in range(8):
        zs[g] = zacc[U * g : U * g + 16, :].astype(BF16)
    z_copies = [
        remote(zs.at[g], zr.at[z], zsend.at[g], zrecv.at[z], owner(g)) for g in range(8)
    ]
    for g in range(8):
        me = same(owner(g))

        @pl.when(jnp.logical_not(me))
        def _():
            z_copies[g].start()

        @pl.when(me)
        def _():
            zr[z] = zs[g]

    for c in y_copies:
        c.wait_recv()
    total = yr[0] + yr[1] + yr[2] + yr[3]
    zsum[...] = total
    s_copies = [
        remote(zsum, zar.at[z], asend.at[i - 1], arecv.at[i - 1], in_z(i))
        for i in range(1, 8)
    ]
    for c in s_copies:
        c.start()
    zar[z] = total

    scale = 1.0 / math.sqrt(32.0 * 32.0 * 32.0)
    for c in s_copies:
        c.wait_recv()
    total = zar[0]
    for i in range(1, 8):
        total = total + zar[i]
    fin[share(gx), :] = total * scale
    l_copies = [
        remote(fin.at[share(gx)], fin.at[share(gx)], qsend.at[i - 1], qrecv.at[i - 1], in_gx(i))
        for i in range(1, 8)
    ]
    for c in l_copies:
        c.start()

    for k in range(8):
        d = source(k)
        got = remote(zs.at[0], zr.at[k], zsend.at[0], zrecv.at[k], d)

        @pl.when(jnp.logical_not(same(d)))
        def _():
            got.wait_recv()

    total = zr[0].astype(F32)
    for k in range(1, 8):
        total = total + zr[k].astype(F32)
    dw_ref[...] = total[0:U, 0:C] * scale

    for c in l_copies:
        c.wait_recv()
    for t in range(CT):
        a0, n = 128 * t, min(128, C - 128 * t)
        for a in range(7):
            row = 56 * t + 8 * a
            kg_ref[a, :, a0 : a0 + n] = fin[row : row + 7, 0:n]
        ng_ref[0:1, a0 : a0 + n] = fin[56 * t + 7 : 56 * t + 8, 0:n]
        ng_ref[1:2, a0 : a0 + n] = fin[56 * t + 15 : 56 * t + 16, 0:n]
    for i in range(HT):
        rp_ref[0:1, 128 * i : 128 * i + 128] = fin[336 + i : 337 + i, :]
        rp_ref[1:2, 128 * i : 128 * i + 128] = fin[360 + i : 361 + i, :]

    x_finish()
    m_finish()

    @pl.when(swap)
    def _():
        swap_u.wait_send()
        o_copy.wait_send()
        o_copy.wait_recv()

    @pl.when(jnp.logical_not(swap))
    def _():
        o_local.wait()

    for c in (
        ni_copies + q_copies + p_copies + a_copies + f_copies
        + r_copies + x_copies + y_copies + s_copies + l_copies
    ):
        c.wait_send()
    for g in range(8):

        @pl.when(jnp.logical_not(same(owner(g))))
        def _():
            z_copies[g].wait_send()


def shards(
    act_codes, act_exponents, grad_codes, grad_exponents, conv_kernel, conv_bias,
    norm_gain, norm_shift, proj_in, proj_bias, response_gain, proj_out,
):
    vmem = pl.BlockSpec(memory_space=pltpu.VMEM)
    hbm = pl.BlockSpec(memory_space=pl.ANY)
    dma = pltpu.SemaphoreType.DMA
    scratch = [
        pltpu.VMEM((CP, H), BF16),
        pltpu.VMEM((CP, H), BF16),
        pltpu.VMEM((7, 8, CP), F32),
        pltpu.VMEM((8, CP), F32),
        pltpu.VMEM((R, W, CP), BF16),
        pltpu.VMEM((R, W, CP), BF16),
        pltpu.VMEM((R + 6, W, CP), BF16),
        pltpu.VMEM((R, W, CP), BF16),
        pltpu.VMEM((R + 6, W, CP), BF16),
        pltpu.VMEM((T, CP), F32),
        pltpu.VMEM((T, CP), F32),
        pltpu.VMEM((T, 128), F32),
        pltpu.VMEM((T, CP), BF16),
        pltpu.VMEM((8, T, CP), BF16),
        pltpu.VMEM((T, H), F32),
        pltpu.VMEM((T, H), F32),
        pltpu.VMEM((T, H), F32),
        pltpu.VMEM((T, H), BF16),
        pltpu.VMEM((H, T), BF16),
        pltpu.VMEM((S, 8 * T), BF16),
        pltpu.VMEM((24, 128), F32),
        pltpu.VMEM((24, 128), F32),
        pltpu.VMEM((8, 24, 128), F32),
        pltpu.VMEM((8, 24, 128), F32),
        pltpu.VMEM((2, 24, 128), F32),
        pltpu.VMEM((S + 8, CP), F32),
        pltpu.VMEM((4, 96, CP), BF16),
        pltpu.VMEM((3, 96, CP), BF16),
        pltpu.VMEM((96, CP), F32),
        pltpu.VMEM((8, 16, CP), BF16),
        pltpu.VMEM((8, 16, CP), BF16),
        pltpu.VMEM((T, CP), F32),
        pltpu.VMEM((R + 6, W, 128), F32),
        pltpu.VMEM((384, 128), F32),
        pltpu.VMEM((8, 48, 128), F32),
        pltpu.VMEM((48, 128), F32),
        pltpu.VMEM((4, 48, 128), F32),
        pltpu.VMEM((48, 128), F32),
        pltpu.VMEM((8, 48, 128), F32),
        pltpu.VMEM((384, 128), F32),
        pltpu.VMEM((R, W, C), BF16),
        dma((2,)),
        dma((1,)),
        dma((2,)), dma((2,)),
        dma((4,)), dma((4,)),
        dma((2, 7)), dma((2, 7)),
        dma((3,)), dma((3,)),
        dma((4,)), dma((4,)),
        dma((7,)), dma((7,)),
        dma((1,)),
        dma((3,)), dma((3,)),
        dma((8,)), dma((8,)),
        dma((7,)), dma((7,)),
        dma((3,)), dma((3,)),
        dma((7,)), dma((7,)),
        dma((7,)), dma((7,)),
        dma((1,)), dma((1,)),
    ]
    outs = pl.pallas_call(
        body,
        out_shape=(
            jax.ShapeDtypeStruct((R, W, C), BF16),
            jax.ShapeDtypeStruct((U, C), F32),
            jax.ShapeDtypeStruct((7, 7, C), F32),
            jax.ShapeDtypeStruct((2, C), F32),
            jax.ShapeDtypeStruct((2, H), F32),
        ),
        in_specs=[vmem] * 8 + [hbm, vmem, vmem, hbm],
        out_specs=(hbm, vmem, vmem, vmem, vmem),
        scratch_shapes=scratch,
        compiler_params=pltpu.CompilerParams(
            collective_id=0, has_side_effects=True, vmem_limit_bytes=56 * 1024 * 1024
        ),
    )(
        act_codes[0],
        act_exponents[0].transpose(2, 0, 1),
        grad_codes[0],
        grad_exponents[0].transpose(2, 0, 1),
        conv_kernel,
        conv_bias.reshape(1, C),
        norm_gain.reshape(1, C),
        norm_shift.reshape(1, C),
        proj_in.T,
        proj_bias.reshape(1, H),
        response_gain.reshape(HT, 128),
        proj_out.T,
    )
    return (outs[0][None],) + tuple(outs[1:])


def solution(mesh):
    strips = P("dp", "rows", None, None)
    return jax.shard_map(
        shards,
        mesh=mesh,
        in_specs=(strips,) * 4 + (P(),) * 8,
        out_specs=(strips, P(("dp", "rows"), None), P(), P(), P()),
        check_vma=False,
    )
```

```python
import math

import jax
import jax.numpy as jnp
from jax import lax
from jax.experimental import pallas as pl
from jax.experimental.pallas import tpu as pltpu
from jax.sharding import PartitionSpec as P

NORM_EPSILON = 1e-06
RESPONSE_EPSILON = 1e-06
HALF_ROOT = 0.7071067811865476
NORMAL_PEAK = 0.3989422804014327

C = 704
CP = 768
CT = CP // 128
H = 2816
HT = H // 128
R = 4
W = 32
T = R * W
S = H // 8
B = S // 4
U = B // 8
F32 = jnp.float32
BF16 = jnp.bfloat16

ALPHA = (
    0.00022905065861350646,
    0.0034082910107109506,
    0.050955695062380861,
    0.18520832239976145,
    1.128379143519084,
)
BETA = (
    -1.1791602954361697e-7,
    0.000023547966471313185,
    0.0010179625278914885,
    0.014070470171167667,
    0.11098505178285362,
    0.49746925110067538,
    1.0,
)


def erf(v):
    v = jnp.clip(v, -3.7439211627767994, 3.7439211627767994)
    s = v * v
    top = jnp.full_like(s, ALPHA[0])
    for c in ALPHA[1:]:
        top = top * s + c
    low = jnp.full_like(s, BETA[0])
    for c in BETA[1:]:
        low = low * s + c
    return v * top / low


class Phases:
    def __init__(self):
        self.scope = None

    def __call__(self, name=None):
        if self.scope is not None:
            self.scope.__exit__(None, None, None)
        self.scope = jax.named_scope(name) if name else None
        if self.scope is not None:
            self.scope.__enter__()


class Post:
    def __init__(self):
        self.leaving, self.coming, self.inside = [], [], []

    @staticmethod
    def under(cond, f):
        if cond is None:
            f()
        else:
            pl.when(cond)(f)

    def send(self, copy, sends=None, receives=None, came=True):
        self.under(sends, copy.start)
        self.leaving.append((copy, sends))
        if came:
            self.coming.append((copy, receives))
        return copy

    def expect(self, copy, receives):
        self.coming.append((copy, receives))
        return copy

    def arrive(self, copies):
        for copy in copies:
            (entry,) = [e for e in self.coming if e[0] is copy]
            self.coming = [e for e in self.coming if e[0] is not copy]
            self.under(entry[1], copy.wait_recv)

    def left(self, copies):
        for copy in copies:
            (entry,) = [e for e in self.leaving if e[0] is copy]
            self.leaving = [e for e in self.leaving if e[0] is not copy]
            self.under(entry[1], copy.wait_send)

    def move(self, copy, cond=None):
        self.under(cond, copy.start)
        self.inside.append((copy, cond))
        return copy

    def moved(self, copies):
        for copy in copies:
            (entry,) = [e for e in self.inside if e[0] is copy]
            self.inside = [e for e in self.inside if e[0] is not copy]
            self.under(entry[1], copy.wait)

    def drain(self):
        self.moved([e[0] for e in self.inside])
        self.arrive([e[0] for e in self.coming])
        self.left([e[0] for e in self.leaving])


def lanes(i, n=128):
    return pl.ds(pl.multiple_of(i * n, n), n)


def moved(v, d):
    if d == 0:
        return v
    w = lax.broadcasted_iota(jnp.int32, v.shape, 0) + d
    return jnp.where((w >= 0) & (w < W), pltpu.roll(v, (-d) % W, 0), 0.0)


def depthwise(rows, weight):
    out = [None] * R
    for b in range(7):
        for r in range(R):
            acc = rows[r] * weight(0, b)
            for a in range(1, 7):
                acc = acc + rows[r + a] * weight(a, b)
            acc = moved(acc, b - 3)
            out[r] = acc if out[r] is None else out[r] + acc
    return out


def body(
    act_ref, aexp_ref, grad_ref, gexp_ref, ck_ref, cb_ref, gain_ref, shift_ref,
    win_hbm, pb_ref, rg_ref, wout_hbm,
    ig_ref, zr, fin,
    win, wout, ckp, prm, sx, su, xs, up, mg, mx, normed, inv, ni, niall,
    act, gp, dg, pg, pgtf, pgt, pgr, stq, stp, rq, rp, coef, dwf, dwp, dwb, xr, zacc, zs,
    ngb, xf, red, redr, ysum, yr, zsum, zar, og,
    wsem, bsem, ssend, srecv, hsend, hrecv, gsend, grecv, nsend, nrecv, fsend, frecv,
    psend, precv, lsem, xsend, xrecv, zsend, zrecv, rsend, rrecv, ysend, yrecv,
    asend, arecv, tsend, trecv, qsend, qrecv, osend, orecv,
):
    phase = Phases()
    post = Post()
    phase("greet")
    dp, rw = lax.axis_index("dp"), lax.axis_index("rows")
    core = lax.rem(dp, 2)
    y = lax.rem(lax.div(dp, 2), 4)
    zl = lax.div(dp, 8)
    x = lax.div(rw, 2)
    zh = lax.rem(rw, 2)
    z = zh * 4 + zl
    gx = 2 * x + core
    gy = 2 * y + core

    def dev(x=x, y=y, zl=zl, zh=zh, core=core):
        return {"dp": (zl * 4 + y) * 2 + core, "rows": x * 2 + zh}

    def in_gx(i):
        m = lax.rem(gx + i, 8)
        return dev(x=lax.div(m, 2), core=lax.rem(m, 2))

    def in_gy(i):
        m = lax.rem(gy + i, 8)
        return dev(y=lax.div(m, 2), core=lax.rem(m, 2)), m

    def in_z(i):
        m = lax.rem(z + i, 8)
        return dev(zl=lax.rem(m, 4), zh=lax.div(m, 4))

    swap = core != zh
    swap_dev = dev(zh=1 - zh, core=1 - core)
    sib = dev(core=1 - core)

    def remote(src, dst, send, recv, to):
        return pltpu.make_async_remote_copy(
            src_ref=src, dst_ref=dst, send_sem=send, recv_sem=recv,
            device_id=to, device_id_type=pl.DeviceIdType.MESH,
        )

    win_copy = pltpu.make_async_copy(win_hbm, win.at[pl.ds(0, C)], wsem.at[0])
    wout_copy = pltpu.make_async_copy(wout_hbm, wout.at[pl.ds(0, C)], wsem.at[1])
    post.move(win_copy)
    post.move(wout_copy)

    barrier = pltpu.get_barrier_semaphore()

    def greet(d):
        pl.semaphore_signal(
            barrier, inc=1, device_id=d, device_id_type=pl.DeviceIdType.MESH
        )

    @pl.when(swap)
    def _():
        greet(swap_dev)

    for i in range(1, 8):
        greet(in_gx(i))
    for i in range(1, 8):
        d, m = in_gy(i)
        greet(d)
    for i in range(1, 8):
        greet(in_z(i))
    guests = 21 + jnp.where(swap, 1, 0)

    phase("scale")
    member = lax.broadcasted_iota(jnp.int32, (C // 32, CP), 1) // 32
    block = lax.broadcasted_iota(jnp.int32, (C // 32, CP), 0)
    spread = jnp.where(member == block, 1.0, 0.0).astype(BF16)

    def scaled(codes, exps, out):
        for r in range(R):
            power = jnp.exp2(exps[:, r, :].astype(F32)).astype(BF16)
            full = lax.dot_general(
                power, spread, (((0,), (0,)), ((), ())), preferred_element_type=F32
            )
            out[r, :, C - 64 : CP] = jnp.zeros((W, CP - C + 64), BF16)
            out[r, :, 0:C] = (codes[r].astype(F32) * full[:, 0:C]).astype(BF16)

    scaled(act_ref, aexp_ref, sx)

    phase("barrier")
    pl.semaphore_wait(barrier, guests)
    phase("scale2")

    swap_x = remote(sx, xs.at[pl.ds(3, R)], ssend.at[0], srecv.at[0], swap_dev)
    swap_u = remote(su, up, ssend.at[1], srecv.at[1], swap_dev)

    post.send(swap_x, swap, swap)
    scaled(grad_ref, gexp_ref, su)

    @pl.when(jnp.logical_not(swap))
    def _():
        xs[3 : 3 + R] = sx[...]
        up[...] = su[...]

    ckp[...] = jnp.zeros_like(ckp)
    prm[...] = jnp.zeros_like(prm)
    ckp[:, 0:7, 0:C] = ck_ref[...]
    prm[0:1, 0:C] = cb_ref[...].reshape(1, C)
    prm[1:2, 0:C] = gain_ref[...].reshape(1, C)
    prm[2:3, 0:C] = shift_ref[...].reshape(1, C)
    win[C:CP, :] = jnp.zeros((CP - C, H), BF16)
    wout[C:CP, :] = jnp.zeros((CP - C, H), BF16)
    first, last = gx == 0, gx == 7

    @pl.when(first)
    def _():
        xs[0:3] = jnp.zeros((3, W, CP), BF16)
        mg[0:3] = jnp.zeros((3, W, CP), BF16)

    @pl.when(last)
    def _():
        xs[7:10] = jnp.zeros((3, W, CP), BF16)
        mg[7:10] = jnp.zeros((3, W, CP), BF16)

    below, above = lax.rem(gx + 1, 8), lax.rem(gx + 7, 8)
    below_dev = dev(x=lax.div(below, 2), core=lax.rem(below, 2))
    above_dev = dev(x=lax.div(above, 2), core=lax.rem(above, 2))

    def halo(buf, base):
        down = remote(buf.at[pl.ds(4, 3)], buf.at[pl.ds(0, 3)],
                      hsend.at[base], hrecv.at[base], below_dev)
        upward = remote(buf.at[pl.ds(3, 3)], buf.at[pl.ds(7, 3)],
                        hsend.at[base + 1], hrecv.at[base + 1], above_dev)

        post.send(down, jnp.logical_not(last), jnp.logical_not(first))
        post.send(upward, jnp.logical_not(first), jnp.logical_not(last))
        return [down, upward]

    phase("swap_wait")
    post.arrive([swap_x])
    phase("halo_wait")
    x_copies = halo(xs, 0)
    post.send(swap_u, swap, swap)
    post.arrive(x_copies)

    phase("conv")
    def conv_tile(t, _):
        at = lanes(t)
        rows = [xs[i, :, at].astype(F32) for i in range(R + 6)]
        out = depthwise(rows, lambda a, b: ckp[a, b : b + 1, at])
        for r in range(R):
            mx[pl.ds(r * W, W), at] = out[r] + prm[0:1, at]
        return 0

    lax.fori_loop(0, CT, conv_tile, 0)

    phase("norm")
    inside = lax.broadcasted_iota(jnp.int32, (W, CP), 1) < C

    def norm_block(r, _):
        at = pl.ds(pl.multiple_of(r * W, W), W)
        v = mx[at, :]
        centered = jnp.where(inside, v - jnp.sum(v, axis=1, keepdims=True) / C, 0.0)
        var = jnp.sum(centered * centered, axis=1, keepdims=True) / C
        inverse = lax.rsqrt(var + NORM_EPSILON)
        n = centered * inverse
        normed[at, :] = n
        inv[at, :] = jnp.broadcast_to(inverse, (W, 128))
        ni[at, :] = (n * prm[1:2, :] + prm[2:3, :]).astype(BF16)
        return 0

    lax.fori_loop(0, R, norm_block, 0)

    ni_copies = []
    for i in range(1, 4):
        to = dev(y=lax.rem(y + i, 4))
        ni_copies.append(
            remote(ni, niall.at[gy], nsend.at[i - 1], nrecv.at[i - 1], to)
        )
    for c in ni_copies:
        post.send(c)
    niall[gy] = ni[...]

    phase("win_wait")
    stq[...] = jnp.zeros_like(stq)
    stp[...] = jnp.zeros_like(stp)
    red[...] = jnp.zeros_like(red)
    post.moved([win_copy])
    phase("active")

    def active(i, _):
        at = lanes(i, 256)
        bias = [pb_ref[pl.ds(2 * i + k, 1), :] for k in range(2)]
        p = jnp.dot(ni[...], win[:, at], preferred_element_type=F32)
        p = p + jnp.concatenate(bias, axis=1)
        phi = 0.5 * (1.0 + erf(p * HALF_ROOT))
        v = p * phi
        act[:, at] = v
        gp[:, at] = phi + p * (NORMAL_PEAK * jnp.exp(-0.5 * p * p))
        s = jnp.sum(v * v, axis=0, keepdims=True)
        stq[pl.ds(2 * i, 1), :] = s[:, 0:128]
        stq[pl.ds(2 * i + 1, 1), :] = s[:, 128:256]
        return 0

    lax.fori_loop(0, HT // 2, active, 0)

    def to_group(src, dst, send, recv):
        return [
            remote(src, dst.at[gx], send.at[i - 1], recv.at[i - 1], in_gx(i))
            for i in range(1, 8)
        ]

    q_copies = to_group(stq, rq, gsend.at[0], grecv.at[0])
    for c in q_copies:
        post.send(c)
    rq[gx] = stq[...]

    phase("up_wait")
    post.arrive([swap_u])
    post.moved([wout_copy])
    phase("down")
    uf = up[...].reshape(T, CP)

    def downward(i, _):
        at = lanes(i, 256)
        d = jnp.dot(uf, wout[:, at], preferred_element_type=F32)
        dg[:, at] = d
        s = jnp.sum(d * act[:, at], axis=0, keepdims=True)
        stp[pl.ds(2 * i, 1), :] = s[:, 0:128]
        stp[pl.ds(2 * i + 1, 1), :] = s[:, 128:256]
        e = jnp.sum(d, axis=0, keepdims=True)
        red[pl.ds(360 + 2 * i, 1), :] = e[:, 0:128]
        red[pl.ds(361 + 2 * i, 1), :] = e[:, 128:256]
        return 0

    lax.fori_loop(0, HT // 2, downward, 0)
    p_copies = to_group(stp, rp, gsend.at[1], grecv.at[1])
    for c in p_copies:
        post.send(c)
    rp[gx] = stp[...]

    phase("response")
    post.arrive(q_copies)
    squares = rq[0, 0:HT]
    for i in range(1, 8):
        squares = squares + rq[i, 0:HT]
    magnitude = jnp.sqrt(squares + RESPONSE_EPSILON)
    denominator = jnp.sum(magnitude) / H + RESPONSE_EPSILON
    response = magnitude / denominator
    coef[0, 0:HT] = 1.0 + rg_ref[...] * response
    red[336 : 336 + HT] = response * stp[0:HT]
    post.arrive(p_copies)
    products = rp[0, 0:HT]
    for i in range(1, 8):
        products = products + rp[i, 0:HT]
    scaled_products = rg_ref[...] * products
    magnitude_grad = scaled_products / denominator - jnp.sum(
        scaled_products * magnitude
    ) / (denominator * denominator * H)
    coef[1, 0:HT] = magnitude_grad / magnitude

    phase("preact")
    own = pl.ds(pl.multiple_of(gy * 128, 128), 128)
    a_copies = [[], []]
    for h in range(2):

        def preact(i, _):
            j = h * (HT // 2) + i
            at = lanes(j)
            a = coef[0, pl.ds(j, 1), :]
            b = coef[1, pl.ds(j, 1), :]
            g = (dg[:, at] * a + act[:, at] * b) * gp[:, at]
            pg[:, at] = g.astype(BF16)
            turned = g.T
            for k in range(16):
                n = i * 16 + k
                q = lax.div(n, B // 8)
                to = (lax.rem(q, 8) * 2 + lax.div(q, 8)) * B + lax.rem(n, B // 8) * 8
                pgtf[pl.ds(pl.multiple_of(to, 8), 8), :] = turned[8 * k : 8 * k + 8, :]
            return 0

        lax.fori_loop(0, HT // 2, preact, 0)
        pgt[h] = pgtf[...].astype(BF16).reshape(8, S // 2, T)
        for i in range(1, 8):
            to, m = in_gy(i)
            copy = remote(
                pgt.at[h, m], pgr.at[h, :, own], psend.at[h, i - 1], precv.at[h, i - 1], to
            )
            a_copies[h].append(post.send(copy))
        pgr[h, :, own] = pgt[h, gy]

    phase("ni_wait")
    post.arrive(ni_copies)
    f_copies = []
    for k in range(4):
        piece = niall.at[2 * k + core]
        f_copies.append(remote(piece, piece, fsend.at[k], frecv.at[k], sib))
    for c in f_copies:
        post.send(c)

    phase("normed_grad")
    ngb[...] = lax.dot_general(
        pg[...], win[...], (((1,), (1,)), ((), ())), preferred_element_type=F32
    )

    phase("norm_grad")

    def norm_grad(r, sums):
        at = pl.ds(pl.multiple_of(r * W, W), W)
        g = ngb[at, :]
        n = normed[at, :]
        gn = g * n
        s = g * prm[1:2, :]
        m1 = jnp.sum(s, axis=1, keepdims=True) / C
        m2 = jnp.sum(s * n, axis=1, keepdims=True) / C
        v = inv[at, :][:, 0:1] * (s - m1 - n * m2)
        mg[3 + r] = jnp.where(inside, v, 0.0).astype(BF16)
        return (
            sums[0] + jnp.sum(gn, axis=0, keepdims=True),
            sums[1] + jnp.sum(g, axis=0, keepdims=True),
        )

    zero = jnp.zeros((1, CP), F32)
    gain_part, shift_part = lax.fori_loop(0, R, norm_grad, (zero, zero))
    m_copies = halo(mg, 2)

    phase("kernel_grad")
    def kernel_tile(t, _):
        at = lanes(t)
        for i in range(R + 6):
            xf[i] = xs[i, :, at].astype(F32)
        g = [mg[3 + r, :, at].astype(F32) for r in range(R)]
        base = t * 56
        for b in range(7):
            gs = [moved(v, 3 - b) for v in g]
            for a in range(7):
                s = xf[a] * gs[0]
                for r in range(1, R):
                    s = s + xf[a + r] * gs[r]
                red[pl.ds(base + a * 8 + b, 1), :] = jnp.sum(s, axis=0, keepdims=True)
        return 0

    lax.fori_loop(0, CT, kernel_tile, 0)
    for t in range(CT):
        red[56 * t + 7 : 56 * t + 8, :] = gain_part[:, 128 * t : 128 * t + 128]
        red[56 * t + 15 : 56 * t + 16, :] = shift_part[:, 128 * t : 128 * t + 128]

    def share(m):
        return pl.ds(pl.multiple_of(m * 64, 8), 64)

    r_copies = []
    for i in range(1, 8):
        m = lax.rem(gx + i, 8)
        r_copies.append(
            remote(red.at[share(m)], redr.at[gx], rsend.at[i - 1], rrecv.at[i - 1], in_gx(i))
        )
    for c in r_copies:
        post.send(c)
    redr[gx] = red[share(gx), :]

    x_copies = [[], []]

    def weight(h):
        phase("pgr_wait%d" % h)
        post.arrive(a_copies[h])
        if h == 0:
            post.arrive(f_copies)
        phase("dw%d" % h)
        dwf[h, S // 2 :, :] = jnp.zeros((8, CP), F32)
        dwf[h, 0 : S // 2, :] = jnp.dot(
            pgr[h], niall[...].reshape(8 * T, CP), preferred_element_type=F32
        )
        for k in range(4):
            part = jnp.concatenate(
                [dwf[h, B * e + 2 * U * k : B * e + 2 * U * k + 24, :] for e in range(2)]
            )
            dwp[h, k] = part
            dwb[h, k] = part.astype(BF16)
        for i in range(1, 4):
            k = lax.rem(x + i, 4)
            copy = remote(
                dwb.at[h, k], xr.at[h, i - 1], xsend.at[h, i - 1], xrecv.at[h, i - 1], dev(x=k)
            )
            x_copies[h].append(post.send(copy))

    def shares(h):
        phase("x_wait%d" % h)
        post.arrive(x_copies[h])
        phase("z_send%d" % h)
        zacc[h, 48:56, :] = jnp.zeros((8, CP), F32)
        total = dwp[h, x]
        for i in range(3):
            total = total + xr[h, i].astype(F32)
        zacc[h, 0:48, :] = total
        for e in range(2):
            for hi in range(2):
                g = (h * 2 + e) * 2 + hi
                zs[g] = zacc[h, 24 * e + U * hi : 24 * e + U * hi + 16, :].astype(BF16)
                to = hi * 4 + h * 2 + e
                copy = remote(
                    zs.at[g], zr.at[z], zsend.at[g], zrecv.at[z],
                    dev(zl=jnp.int32(h * 2 + e), zh=jnp.int32(hi)),
                )
                post.send(copy, z != to, came=False)

                @pl.when(z == to)
                def _():
                    zr[z] = zs[g]

    weight(0)

    phase("m_wait")
    post.arrive(m_copies)
    phase("back")

    def back_tile(t, _):
        at = lanes(t)
        rows = [mg[i, :, at].astype(F32) for i in range(R + 6)]
        out = depthwise(rows, lambda a, b: ckp[6 - a, 6 - b : 7 - b, at])
        for r in range(R):
            sx[r, :, at] = (out[r] + up[r, :, at].astype(F32)).astype(BF16)
        return 0

    post.left([swap_x])
    lax.fori_loop(0, CT, back_tile, 0)
    og[...] = sx[:, :, 0:C]
    o_copy = remote(og, ig_ref, osend.at[0], orecv.at[0], swap_dev)
    o_local = pltpu.make_async_copy(og, ig_ref, lsem.at[0])
    post.send(o_copy, swap, swap)
    post.move(o_local, jnp.logical_not(swap))

    phase("r_wait")
    post.arrive(r_copies)
    total = redr[0]
    for i in range(1, 8):
        total = total + redr[i]
    ysum[...] = total.reshape(4, 16, 128)
    y_copies = []
    for i in range(1, 4):
        k = lax.rem(y + i, 4)
        copy = remote(ysum.at[k], yr.at[y], ysend.at[i - 1], yrecv.at[i - 1], dev(y=k))
        y_copies.append(post.send(copy))
    yr[y] = ysum[y]

    weight(1)
    phase("y_wait")
    post.arrive(y_copies)
    total = yr[0] + yr[1] + yr[2] + yr[3]
    zsum[...] = total
    s_copies = [
        remote(zsum, zar.at[z], asend.at[i - 1], arecv.at[i - 1], in_z(i))
        for i in range(1, 8)
    ]
    for c in s_copies:
        post.send(c)
    zar[z] = total

    shares(0)
    shares(1)
    z_comes = []
    for k in range(8):
        got = remote(
            zs.at[0], zr.at[k], zsend.at[0], zrecv.at[k],
            dev(zl=jnp.int32(k % 4), zh=jnp.int32(k // 4)),
        )
        z_comes.append(post.expect(got, z != k))

    phase("s_wait")
    post.arrive(s_copies)
    total = zar[0]
    for i in range(1, 8):
        total = total + zar[i]
    mine = pl.ds(pl.multiple_of(gx * 64 + y * 16, 8), 16)
    fin[mine, :] = total
    h_copies = [
        remote(fin.at[mine], fin.at[mine], tsend.at[i - 1], trecv.at[i - 1],
               dev(y=lax.rem(y + i, 4)))
        for i in range(1, 4)
    ]
    for c in h_copies:
        post.send(c)
    phase("h_wait")
    post.arrive(h_copies)
    l_copies = [
        remote(fin.at[share(gx)], fin.at[share(gx)], qsend.at[i - 1], qrecv.at[i - 1], in_gx(i))
        for i in range(1, 8)
    ]
    for c in l_copies:
        post.send(c)
    phase("z_wait")
    post.arrive(z_comes)
    phase("l_wait")
    post.arrive(l_copies)
    phase("o_wait")
    post.arrive([o_copy])
    post.moved([o_local])

    phase("sends")
    post.drain()
    phase()


def finish(ig_ref, zr, fin, out_ref, dw_ref, kg_ref, ng_ref, rp_ref):
    out_ref[...] = ig_ref[...]
    scale = 1.0 / math.sqrt(32.0 * 32.0 * 32.0)
    total = zr[0].astype(F32)
    for k in range(1, 8):
        total = total + zr[k].astype(F32)
    dw_ref[...] = total[0:U, 0:C] * scale
    for t in range(CT):
        a0, n = 128 * t, min(128, C - 128 * t)
        for a in range(7):
            row = 56 * t + 8 * a
            kg_ref[a, :, a0 : a0 + n] = fin[row : row + 7, 0:n] * scale
        ng_ref[0:1, a0 : a0 + n] = fin[56 * t + 7 : 56 * t + 8, 0:n] * scale
        ng_ref[1:2, a0 : a0 + n] = fin[56 * t + 15 : 56 * t + 16, 0:n] * scale
    for i in range(HT):
        rp_ref[0:1, 128 * i : 128 * i + 128] = fin[336 + i : 337 + i, :] * scale
        rp_ref[1:2, 128 * i : 128 * i + 128] = fin[360 + i : 361 + i, :] * scale


def shards(
    act_codes, act_exponents, grad_codes, grad_exponents, conv_kernel, conv_bias,
    norm_gain, norm_shift, proj_in, proj_bias, response_gain, proj_out,
):
    vmem = pl.BlockSpec(memory_space=pltpu.VMEM)
    hbm = pl.BlockSpec(memory_space=pl.ANY)
    dma = pltpu.SemaphoreType.DMA
    scratch = [
        pltpu.VMEM((CP, H), BF16),
        pltpu.VMEM((CP, H), BF16),
        pltpu.VMEM((7, 8, CP), F32),
        pltpu.VMEM((8, CP), F32),
        pltpu.VMEM((R, W, CP), BF16),
        pltpu.VMEM((R, W, CP), BF16),
        pltpu.VMEM((R + 6, W, CP), BF16),
        pltpu.VMEM((R, W, CP), BF16),
        pltpu.VMEM((R + 6, W, CP), BF16),
        pltpu.VMEM((T, CP), F32),
        pltpu.VMEM((T, CP), F32),
        pltpu.VMEM((T, 128), F32),
        pltpu.VMEM((T, CP), BF16),
        pltpu.VMEM((8, T, CP), BF16),
        pltpu.VMEM((T, H), F32),
        pltpu.VMEM((T, H), F32),
        pltpu.VMEM((T, H), F32),
        pltpu.VMEM((T, H), BF16),
        pltpu.VMEM((H // 2, T), F32),
        pltpu.VMEM((2, 8, S // 2, T), BF16),
        pltpu.VMEM((2, S // 2, 8 * T), BF16),
        pltpu.VMEM((24, 128), F32),
        pltpu.VMEM((24, 128), F32),
        pltpu.VMEM((8, 24, 128), F32),
        pltpu.VMEM((8, 24, 128), F32),
        pltpu.VMEM((2, 24, 128), F32),
        pltpu.VMEM((2, S // 2 + 8, CP), F32),
        pltpu.VMEM((2, 4, 48, CP), F32),
        pltpu.VMEM((2, 4, 48, CP), BF16),
        pltpu.VMEM((2, 3, 48, CP), BF16),
        pltpu.VMEM((2, 56, CP), F32),
        pltpu.VMEM((8, 16, CP), BF16),
        pltpu.VMEM((T, CP), F32),
        pltpu.VMEM((R + 6, W, 128), F32),
        pltpu.VMEM((512, 128), F32),
        pltpu.VMEM((8, 64, 128), F32),
        pltpu.VMEM((4, 16, 128), F32),
        pltpu.VMEM((4, 16, 128), F32),
        pltpu.VMEM((16, 128), F32),
        pltpu.VMEM((8, 16, 128), F32),
        pltpu.VMEM((R, W, C), BF16),
        dma((2,)),
        dma((1,)),
        dma((2,)), dma((2,)),
        dma((4,)), dma((4,)),
        dma((2, 7)), dma((2, 7)),
        dma((3,)), dma((3,)),
        dma((4,)), dma((4,)),
        dma((2, 7)), dma((2, 7)),
        dma((1,)),
        dma((2, 3)), dma((2, 3)),
        dma((8,)), dma((8,)),
        dma((7,)), dma((7,)),
        dma((3,)), dma((3,)),
        dma((7,)), dma((7,)),
        dma((3,)), dma((3,)),
        dma((7,)), dma((7,)),
        dma((1,)), dma((1,)),
    ]
    outs = pl.pallas_call(
        body,
        out_shape=(
            jax.ShapeDtypeStruct((R, W, C), BF16),
            jax.ShapeDtypeStruct((8, 16, CP), BF16),
            jax.ShapeDtypeStruct((512, 128), F32),
        ),
        in_specs=[vmem] * 8 + [hbm, vmem, vmem, hbm],
        out_specs=(hbm, vmem, vmem),
        scratch_shapes=scratch,
        compiler_params=pltpu.CompilerParams(
            collective_id=0, has_side_effects=True, vmem_limit_bytes=56 * 1024 * 1024
        ),
    )(
        act_codes[0],
        act_exponents[0].transpose(2, 0, 1),
        grad_codes[0],
        grad_exponents[0].transpose(2, 0, 1),
        conv_kernel,
        conv_bias,
        norm_gain,
        norm_shift,
        proj_in.T,
        proj_bias.reshape(HT, 128),
        response_gain.reshape(HT, 128),
        proj_out.T,
    )
    results = pl.pallas_call(
        finish,
        out_shape=(
            jax.ShapeDtypeStruct((R, W, C), BF16),
            jax.ShapeDtypeStruct((U, C), F32),
            jax.ShapeDtypeStruct((7, 7, C), F32),
            jax.ShapeDtypeStruct((2, C), F32),
            jax.ShapeDtypeStruct((2, H), F32),
        ),
        in_specs=[vmem] * 3,
        out_specs=(vmem,) * 5,
    )(*outs)
    return (results[0][None],) + tuple(results[1:])


def solution(mesh):
    strips = P("dp", "rows", None, None)
    return jax.shard_map(
        shards,
        mesh=mesh,
        in_specs=(strips,) * 4 + (P(),) * 8,
        out_specs=(strips, P(("dp", "rows"), None), P(), P(), P()),
        check_vma=False,
    )
```

```python
import math

import jax
import jax.numpy as jnp
from jax import lax
from jax.experimental import pallas as pl
from jax.experimental.pallas import tpu as pltpu
from jax.sharding import PartitionSpec as P

NORM_EPSILON = 1e-06
RESPONSE_EPSILON = 1e-06
HALF_ROOT = 0.7071067811865476
NORMAL_PEAK = 0.3989422804014327

C = 704
CP = 768
CT = CP // 128
H = 2816
HT = H // 128
R = 4
W = 32
T = R * W
S = H // 8
B = S // 4
U = B // 8
F32 = jnp.float32
BF16 = jnp.bfloat16

ALPHA = (
    0.00022905065861350646,
    0.0034082910107109506,
    0.050955695062380861,
    0.18520832239976145,
    1.128379143519084,
)
BETA = (
    -1.1791602954361697e-7,
    0.000023547966471313185,
    0.0010179625278914885,
    0.014070470171167667,
    0.11098505178285362,
    0.49746925110067538,
    1.0,
)


def erf(v):
    v = jnp.clip(v, -3.7439211627767994, 3.7439211627767994)
    s = v * v
    top = jnp.full_like(s, ALPHA[0])
    for c in ALPHA[1:]:
        top = top * s + c
    low = jnp.full_like(s, BETA[0])
    for c in BETA[1:]:
        low = low * s + c
    return v * top / low


class Phases:
    def __init__(self):
        self.scope = None

    def __call__(self, name=None):
        if self.scope is not None:
            self.scope.__exit__(None, None, None)
        self.scope = jax.named_scope(name) if name else None
        if self.scope is not None:
            self.scope.__enter__()


class Post:
    def __init__(self):
        self.leaving, self.coming, self.inside = [], [], []

    @staticmethod
    def under(cond, f):
        if cond is None:
            f()
        else:
            pl.when(cond)(f)

    def send(self, copy, sends=None, receives=None, came=True):
        self.under(sends, copy.start)
        self.leaving.append((copy, sends))
        if came:
            self.coming.append((copy, receives))
        return copy

    def together(self, copies, whole, sends=None):
        sends = sends or [None] * len(copies)
        for copy, cond in zip(copies, sends, strict=True):
            self.under(cond, copy.start)
        if whole is not None:
            self.leaving.append((whole, None))
            self.coming.append((whole, None))
        return [whole]

    def arrive(self, copies):
        for copy in copies:
            (entry,) = [e for e in self.coming if e[0] is copy]
            self.coming = [e for e in self.coming if e[0] is not copy]
            self.under(entry[1], copy.wait_recv)

    def left(self, copies):
        for copy in copies:
            (entry,) = [e for e in self.leaving if e[0] is copy]
            self.leaving = [e for e in self.leaving if e[0] is not copy]
            self.under(entry[1], copy.wait_send)

    def move(self, copy, cond=None):
        self.under(cond, copy.start)
        self.inside.append((copy, cond))
        return copy

    def moved(self, copies):
        for copy in copies:
            (entry,) = [e for e in self.inside if e[0] is copy]
            self.inside = [e for e in self.inside if e[0] is not copy]
            self.under(entry[1], copy.wait)

    def drain(self):
        self.moved([e[0] for e in self.inside])
        self.arrive([e[0] for e in self.coming])
        self.left([e[0] for e in self.leaving])


def lanes(i, n=128):
    return pl.ds(pl.multiple_of(i * n, n), n)


def moved(v, d):
    if d == 0:
        return v
    w = lax.broadcasted_iota(jnp.int32, v.shape, 0) + d
    return jnp.where((w >= 0) & (w < W), pltpu.roll(v, (-d) % W, 0), 0.0)


def depthwise(rows, weight):
    out = [None] * R
    for b in range(7):
        for r in range(R):
            acc = rows[r] * weight(0, b)
            for a in range(1, 7):
                acc = acc + rows[r + a] * weight(a, b)
            acc = moved(acc, b - 3)
            out[r] = acc if out[r] is None else out[r] + acc
    return out


def body(
    act_in, aexp_in, grad_in, gexp_in, ck_in, cb_in, gain_in, shift_in,
    win_hbm, pb_in, rg_in, wout_hbm,
    ig_ref, zr, fin,
    act_ref, aexp_ref, grad_ref, gexp_ref, ck_ref, cb_ref, gain_ref, shift_ref, pb_ref, rg_ref,
    win, wout, ckp, prm, sx, su, xs, up, mg, mx, normed, inv, ni, niall,
    act, gp, dg, pg, pgtf, pgt, pgr, stq, stp, rq, rp, coef, dwf, dwp, dwb, xr, zacc, zs,
    ngb, xf, red, redr, zsum, zar, back, og,
    wsem, isem, ssend, srecv, hsend, hrecv, gsend, grecv, nsend, nrecv, fsend, frecv,
    psend, precv, lsem, xsend, xrecv, zsend, zrecv, rsend, rrecv,
    zlocal, asend, arecv, qsend, qrecv, osend, orecv,
):
    phase = Phases()
    post = Post()
    phase("greet")
    dp, rw = lax.axis_index("dp"), lax.axis_index("rows")
    core = lax.rem(dp, 2)
    y = lax.rem(lax.div(dp, 2), 4)
    zl = lax.div(dp, 8)
    x = lax.div(rw, 2)
    zh = lax.rem(rw, 2)
    z = zh * 4 + zl
    gx = 2 * x + core
    gy = 2 * y + core

    def dev(x=x, y=y, zl=zl, zh=zh, core=core):
        return {"dp": (zl * 4 + y) * 2 + core, "rows": x * 2 + zh}

    def in_gx(i):
        m = lax.rem(gx + i, 8)
        return dev(x=lax.div(m, 2), core=lax.rem(m, 2))

    def in_gy(i):
        m = lax.rem(gy + i, 8)
        return dev(y=lax.div(m, 2), core=lax.rem(m, 2)), m

    def in_layer(iy, i):
        m, yy = lax.rem(gx + i, 8), lax.rem(y + iy, 4)
        return dev(x=lax.div(m, 2), core=lax.rem(m, 2), y=yy), m, yy

    layer = [(iy, i) for iy in range(4) for i in range(8)][1:]

    def in_z(i):
        m = lax.rem(z + i, 8)
        return dev(zl=lax.rem(m, 4), zh=lax.div(m, 4))

    swap = core != zh
    swap_dev = dev(zh=1 - zh, core=1 - core)
    sib = dev(core=1 - core)

    def remote(src, dst, send, recv, to):
        return pltpu.make_async_remote_copy(
            src_ref=src, dst_ref=dst, send_sem=send, recv_sem=recv,
            device_id=to, device_id_type=pl.DeviceIdType.MESH,
        )

    loads = [
        pltpu.make_async_copy(a, b, isem.at[k])
        for k, (a, b) in enumerate(
            (
                (aexp_in, aexp_ref), (act_in, act_ref), (gexp_in, gexp_ref), (grad_in, grad_ref),
                (ck_in, ck_ref), (cb_in, cb_ref), (gain_in, gain_ref), (shift_in, shift_ref),
                (pb_in, pb_ref), (rg_in, rg_ref),
            )
        )
    ]
    win_copy = pltpu.make_async_copy(win_hbm, win.at[pl.ds(0, C)], wsem.at[0])
    wout_copy = pltpu.make_async_copy(wout_hbm, wout.at[pl.ds(0, C)], wsem.at[1])

    barrier = pltpu.get_barrier_semaphore()

    def greet(d):
        pl.semaphore_signal(
            barrier, inc=1, device_id=d, device_id_type=pl.DeviceIdType.MESH
        )

    @pl.when(swap)
    def _():
        greet(swap_dev)

    for iy, i in layer:
        greet(in_layer(iy, i)[0])
    for i in range(1, 8):
        greet(in_z(i))
    guests = 38 + jnp.where(swap, 1, 0)

    for c in loads + [win_copy, wout_copy]:
        post.move(c)
    phase("scale")
    member = lax.broadcasted_iota(jnp.int32, (C // 32, CP), 1) // 32
    block = lax.broadcasted_iota(jnp.int32, (C // 32, CP), 0)
    spread = jnp.where(member == block, 1.0, 0.0).astype(BF16)

    def scaled(codes, exps, out):
        for r in range(R):
            power = jnp.exp2(exps[:, r, :].astype(F32)).astype(BF16)
            full = lax.dot_general(
                power, spread, (((0,), (0,)), ((), ())), preferred_element_type=F32
            )
            out[r, :, C - 64 : CP] = jnp.zeros((W, CP - C + 64), BF16)
            out[r, :, 0:C] = (codes[r].astype(F32) * full[:, 0:C]).astype(BF16)

    post.moved(loads[0:2])
    scaled(act_ref, aexp_ref, sx)

    phase("barrier")
    pl.semaphore_wait(barrier, guests)
    phase("scale2")

    thirds = [pl.ds(CP // 3 * k, CP // 3) for k in range(3)]
    swap_x = [
        remote(sx.at[:, :, at], xs.at[pl.ds(3, R), :, at], ssend.at[k], srecv.at[k], swap_dev)
        for k, at in enumerate(thirds)
    ]
    swap_u = remote(su, up, ssend.at[3], srecv.at[3], swap_dev)

    post.send(swap_x[0], swap, swap)
    post.moved(loads[2:])
    scaled(grad_ref, gexp_ref, su)

    @pl.when(jnp.logical_not(swap))
    def _():
        xs[3 : 3 + R] = sx[...]
        up[...] = su[...]

    ckp[...] = jnp.zeros_like(ckp)
    prm[...] = jnp.zeros_like(prm)
    ckp[:, 0:7, 0:C] = ck_ref[...]
    prm[0:1, 0:C] = cb_ref[...].reshape(1, C)
    prm[1:2, 0:C] = gain_ref[...].reshape(1, C)
    prm[2:3, 0:C] = shift_ref[...].reshape(1, C)
    win[C:CP, :] = jnp.zeros((CP - C, H), BF16)
    wout[C:CP, :] = jnp.zeros((CP - C, H), BF16)
    first, last = gx == 0, gx == 7

    @pl.when(first)
    def _():
        xs[0:3] = jnp.zeros((3, W, CP), BF16)
        mg[0:3] = jnp.zeros((3, W, CP), BF16)

    @pl.when(last)
    def _():
        xs[7:10] = jnp.zeros((3, W, CP), BF16)
        mg[7:10] = jnp.zeros((3, W, CP), BF16)

    below, above = lax.rem(gx + 1, 8), lax.rem(gx + 7, 8)
    below_dev = dev(x=lax.div(below, 2), core=lax.rem(below, 2))
    above_dev = dev(x=lax.div(above, 2), core=lax.rem(above, 2))

    def halo(buf, base, at=slice(None)):
        down = remote(buf.at[pl.ds(4, 3), :, at], buf.at[pl.ds(0, 3), :, at],
                      hsend.at[base], hrecv.at[base], below_dev)
        upward = remote(buf.at[pl.ds(3, 3), :, at], buf.at[pl.ds(7, 3), :, at],
                        hsend.at[base + 1], hrecv.at[base + 1], above_dev)

        post.send(down, jnp.logical_not(last), jnp.logical_not(first))
        post.send(upward, jnp.logical_not(first), jnp.logical_not(last))
        return [down, upward]

    def conv_tile(t, _):
        at = lanes(t)
        rows = [xs[i, :, at].astype(F32) for i in range(R + 6)]
        out = depthwise(rows, lambda a, b: ckp[a, b : b + 1, at])
        for r in range(R):
            mx[pl.ds(r * W, W), at] = out[r] + prm[0:1, at]
        return 0

    near = []
    for k in range(4):
        if k < 3:
            phase("swap_wait%d" % k)
            post.left([swap_x[k]])
            if k < 2:
                post.send(swap_x[k + 1], swap, swap)
            else:
                post.send(swap_u, swap, swap)
            post.arrive([swap_x[k]])
            near.append(halo(xs, 2 * k, thirds[k]))
        if k > 0:
            phase("halo_wait%d" % (k - 1))
            post.arrive(near[k - 1])
            phase("conv%d" % (k - 1))
            lax.fori_loop((k - 1) * CT // 3, k * CT // 3, conv_tile, 0)
    phase("norm")
    inside = lax.broadcasted_iota(jnp.int32, (W, CP), 1) < C

    def norm_block(r, _):
        at = pl.ds(pl.multiple_of(r * W, W), W)
        v = mx[at, :]
        centered = jnp.where(inside, v - jnp.sum(v, axis=1, keepdims=True) / C, 0.0)
        var = jnp.sum(centered * centered, axis=1, keepdims=True) / C
        inverse = lax.rsqrt(var + NORM_EPSILON)
        n = centered * inverse
        normed[at, :] = n
        inv[at, :] = jnp.broadcast_to(inverse, (W, 128))
        ni[at, :] = (n * prm[1:2, :] + prm[2:3, :]).astype(BF16)
        return 0

    lax.fori_loop(0, R, norm_block, 0)

    three = niall.at[pl.ds(0, 3)]
    ni_copies = post.together(
        [
            remote(ni, niall.at[gy], nsend, nrecv, dev(y=lax.rem(y + i, 4)))
            for i in range(1, 4)
        ],
        remote(three, three, nsend, nrecv, sib),
    )
    niall[gy] = ni[...]

    phase("win_wait")
    stq[...] = jnp.zeros_like(stq)
    stp[...] = jnp.zeros_like(stp)
    red[...] = jnp.zeros_like(red)
    post.moved([win_copy])
    phase("active")

    def active(i, _):
        at = lanes(i, 256)
        bias = [pb_ref[pl.ds(2 * i + k, 1), :] for k in range(2)]
        p = jnp.dot(ni[...], win[:, at], preferred_element_type=F32)
        p = p + jnp.concatenate(bias, axis=1)
        phi = 0.5 * (1.0 + erf(p * HALF_ROOT))
        v = p * phi
        act[:, at] = v
        gp[:, at] = phi + p * (NORMAL_PEAK * jnp.exp(-0.5 * p * p))
        s = jnp.sum(v * v, axis=0, keepdims=True)
        stq[pl.ds(2 * i, 1), :] = s[:, 0:128]
        stq[pl.ds(2 * i + 1, 1), :] = s[:, 128:256]
        return 0

    lax.fori_loop(0, HT // 2, active, 0, unroll=True)

    def to_group(src, dst, send, recv):
        seven = dst.at[pl.ds(0, 7)]
        return post.together(
            [remote(src, dst.at[gx], send, recv, in_gx(i)) for i in range(1, 8)],
            remote(seven, seven, send, recv, sib),
        )

    q_copies = to_group(stq, rq, gsend.at[0], grecv.at[0])
    rq[gx] = stq[...]

    phase("up_wait")
    post.arrive([swap_u])
    post.moved([wout_copy])
    phase("down")
    uf = up[...].reshape(T, CP)

    dg[...] = jnp.dot(uf, wout[...], preferred_element_type=F32)

    def downward(i, _):
        at = lanes(i, 256)
        d = dg[:, at]
        s = jnp.sum(d * act[:, at], axis=0, keepdims=True)
        stp[pl.ds(2 * i, 1), :] = s[:, 0:128]
        stp[pl.ds(2 * i + 1, 1), :] = s[:, 128:256]
        e = jnp.sum(d, axis=0, keepdims=True)
        red[pl.ds(360 + 2 * i, 1), :] = e[:, 0:128]
        red[pl.ds(361 + 2 * i, 1), :] = e[:, 128:256]
        return 0

    lax.fori_loop(0, HT // 2, downward, 0, unroll=True)
    p_copies = to_group(stp, rp, gsend.at[1], grecv.at[1])
    rp[gx] = stp[...]

    phase("response")
    post.arrive(q_copies)
    squares = rq[0, 0:HT]
    for i in range(1, 8):
        squares = squares + rq[i, 0:HT]
    magnitude = jnp.sqrt(squares + RESPONSE_EPSILON)
    denominator = jnp.sum(magnitude) / H + RESPONSE_EPSILON
    response = magnitude / denominator
    coef[0, 0:HT] = 1.0 + rg_ref[...] * response
    red[336 : 336 + HT] = response * stp[0:HT]
    post.arrive(p_copies)
    products = rp[0, 0:HT]
    for i in range(1, 8):
        products = products + rp[i, 0:HT]
    scaled_products = rg_ref[...] * products
    magnitude_grad = scaled_products / denominator - jnp.sum(
        scaled_products * magnitude
    ) / (denominator * denominator * H)
    coef[1, 0:HT] = magnitude_grad / magnitude

    phase("preact")
    own = pl.ds(pl.multiple_of(gy * 128, 128), 128)
    a_copies = [[], []]
    for h in range(2):

        def preact(i, _):
            j = h * (HT // 2) + i
            at = lanes(j)
            a = coef[0, pl.ds(j, 1), :]
            b = coef[1, pl.ds(j, 1), :]
            g = (dg[:, at] * a + act[:, at] * b) * gp[:, at]
            pg[:, at] = g.astype(BF16)
            turned = g.T
            for k in range(16):
                n = i * 16 + k
                q = lax.div(n, B // 8)
                to = (lax.rem(q, 8) * 2 + lax.div(q, 8)) * B + lax.rem(n, B // 8) * 8
                pgtf[pl.ds(pl.multiple_of(to, 8), 8), :] = turned[8 * k : 8 * k + 8, :]
            return 0

        lax.fori_loop(0, HT // 2, preact, 0, unroll=True)
        pgt[h] = pgtf[...].astype(BF16).reshape(8, S // 2, T)
        copies = []
        for i in range(1, 8):
            to, m = in_gy(i)
            copies.append(
                remote(pgt.at[h, m], pgr.at[h, :, own], psend.at[h], precv.at[h], to)
            )
        seven = pgt.at[h, pl.ds(0, 7)]
        a_copies[h] = post.together(
            copies, remote(seven, seven, psend.at[h], precv.at[h], sib)
        )
        pgr[h, :, own] = pgt[h, gy]

    phase("normed_grad")
    ngb[...] = lax.dot_general(
        pg[...], win[...], (((1,), (1,)), ((), ())), preferred_element_type=F32
    )

    phase("ni_wait")
    post.arrive(ni_copies)
    pieces = [niall.at[2 * k + core] for k in range(4)]
    four = niall.at[pl.ds(0, 4)]
    f_copies = post.together(
        [remote(p, p, fsend, frecv, sib) for p in pieces],
        remote(four, four, fsend, frecv, sib),
    )

    phase("norm_grad")

    def norm_grad(r, sums):
        at = pl.ds(pl.multiple_of(r * W, W), W)
        g = ngb[at, :]
        n = normed[at, :]
        gn = g * n
        s = g * prm[1:2, :]
        m1 = jnp.sum(s, axis=1, keepdims=True) / C
        m2 = jnp.sum(s * n, axis=1, keepdims=True) / C
        v = inv[at, :][:, 0:1] * (s - m1 - n * m2)
        mg[3 + r] = jnp.where(inside, v, 0.0).astype(BF16)
        return (
            sums[0] + jnp.sum(gn, axis=0, keepdims=True),
            sums[1] + jnp.sum(g, axis=0, keepdims=True),
        )

    zero = jnp.zeros((1, CP), F32)
    gain_part, shift_part = lax.fori_loop(0, R, norm_grad, (zero, zero))
    m_copies = halo(mg, 6)

    phase("kernel_grad")
    def kernel_tile(t, _):
        at = lanes(t)
        for i in range(R + 6):
            xf[i] = xs[i, :, at].astype(F32)
        g = [mg[3 + r, :, at].astype(F32) for r in range(R)]
        base = t * 56
        for b in range(7):
            gs = [moved(v, 3 - b) for v in g]
            for a in range(7):
                s = xf[a] * gs[0]
                for r in range(1, R):
                    s = s + xf[a + r] * gs[r]
                red[pl.ds(base + a * 8 + b, 1), :] = jnp.sum(s, axis=0, keepdims=True)
        return 0

    lax.fori_loop(0, CT, kernel_tile, 0)
    for t in range(CT):
        red[56 * t + 7 : 56 * t + 8, :] = gain_part[:, 128 * t : 128 * t + 128]
        red[56 * t + 15 : 56 * t + 16, :] = shift_part[:, 128 * t : 128 * t + 128]

    def piece(m, yy):
        return pl.ds(pl.multiple_of(m * 64 + yy * 16, 8), 16)

    mine = piece(gx, y)
    place = gx * 4 + y
    copies = []
    for iy, i in layer:
        to, m, yy = in_layer(iy, i)
        copies.append(remote(red.at[piece(m, yy)], redr.at[place], rsend, rrecv, to))
    most = redr.at[pl.ds(0, 31)]
    r_copies = post.together(copies, remote(most, most, rsend, rrecv, sib))
    redr[place] = red[mine, :]

    x_copies = [[], []]

    def weight(h):
        phase("pgr_wait%d" % h)
        post.arrive(a_copies[h])
        if h == 0:
            post.arrive(f_copies)
        phase("dw%d" % h)
        dwf[h, S // 2 :, :] = jnp.zeros((8, CP), F32)
        dwf[h, 0 : S // 2, :] = jnp.dot(
            pgr[h], niall[...].reshape(8 * T, CP), preferred_element_type=F32
        )
        for k in range(4):
            part = jnp.concatenate(
                [dwf[h, B * e + 2 * U * k : B * e + 2 * U * k + 24, :] for e in range(2)]
            )
            dwp[h, k] = part
            dwb[h, k] = part.astype(BF16)
        copies = []
        for i in range(1, 4):
            k = lax.rem(x + i, 4)
            copies.append(
                remote(dwb.at[h, k], xr.at[h, i - 1], xsend.at[h], xrecv.at[h], dev(x=k))
            )
        x_copies[h] = post.together(
            copies, remote(xr.at[h], xr.at[h], xsend.at[h], xrecv.at[h], sib)
        )

    def shares(h):
        phase("x_wait%d" % h)
        post.arrive(x_copies[h])
        phase("z_send%d" % h)
        zacc[h, 48:56, :] = jnp.zeros((8, CP), F32)
        total = dwp[h, x]
        for i in range(3):
            total = total + xr[h, i].astype(F32)
        zacc[h, 0:48, :] = total
        for e in range(2):
            for hi in range(2):
                g = (h * 2 + e) * 2 + hi
                zs[g] = zacc[h, 24 * e + U * hi : 24 * e + U * hi + 16, :].astype(BF16)
                to = hi * 4 + h * 2 + e
                copy = remote(
                    zs.at[g], zr.at[z], zsend, zrecv,
                    dev(zl=jnp.int32(h * 2 + e), zh=jnp.int32(hi)),
                )
                post.together([copy], None, [z != to])
                own_share = pltpu.make_async_copy(zs.at[g], zr.at[z], zlocal)
                pl.when(z == to)(own_share.start)

    weight(0)

    phase("m_wait")
    post.arrive(m_copies)
    phase("back")

    def back_tile(t, _):
        at = lanes(t)
        rows = [mg[i, :, at].astype(F32) for i in range(R + 6)]
        out = depthwise(rows, lambda a, b: ckp[6 - a, 6 - b : 7 - b, at])
        for r in range(R):
            sx[r, :, at] = (out[r] + up[r, :, at].astype(F32)).astype(BF16)
        return 0

    lax.fori_loop(0, CT, back_tile, 0)
    og[...] = sx[:, :, 0:C]
    o_copy = remote(og, ig_ref, osend.at[0], orecv.at[0], swap_dev)
    o_local = pltpu.make_async_copy(og, ig_ref, lsem.at[0])

    post.send(o_copy, swap, swap)
    post.move(o_local, jnp.logical_not(swap))
    weight(1)

    phase("r_wait")
    post.arrive(r_copies)
    total = redr[0]
    for i in range(1, 32):
        total = total + redr[i]
    zsum[...] = total
    seven = zar.at[pl.ds(0, 7)]
    s_copies = post.together(
        [remote(zsum, zar.at[z], asend, arecv, in_z(i)) for i in range(1, 8)],
        remote(seven, seven, asend, arecv, sib),
    )
    zar[z] = total

    shares(0)

    phase("s_wait")
    post.arrive(s_copies)
    total = zar[0]
    for i in range(1, 8):
        total = total + zar[i]
    back[...] = total
    l_copies = post.together(
        [
            remote(back, fin.at[mine], qsend, qrecv, in_layer(iy, i)[0])
            for iy, i in layer
        ],
        remote(most, most, qsend, qrecv, sib),
    )
    own_sums = post.move(pltpu.make_async_copy(back, fin.at[mine], lsem.at[1]))
    shares(1)
    seven = zs.at[pl.ds(0, 7)]
    z_comes = post.together([], remote(seven, seven, zsend, zrecv, sib))
    phase("z_wait")
    post.arrive(z_comes)
    phase("l_wait")
    post.arrive(l_copies)
    phase("o_wait")
    post.arrive([o_copy])
    post.moved([o_local, own_sums])
    pltpu.make_async_copy(zs.at[0], zr.at[z], zlocal).wait()

    phase("sends")
    post.drain()
    phase()


def finish(ig_ref, zr, fin, out_ref, dw_ref, kg_ref, ng_ref, rp_ref):
    out_ref[...] = ig_ref[...]
    scale = 1.0 / math.sqrt(32.0 * 32.0 * 32.0)
    total = zr[0].astype(F32)
    for k in range(1, 8):
        total = total + zr[k].astype(F32)
    dw_ref[...] = total[0:U, 0:C] * scale
    for t in range(CT):
        a0, n = 128 * t, min(128, C - 128 * t)
        for a in range(7):
            row = 56 * t + 8 * a
            kg_ref[a, :, a0 : a0 + n] = fin[row : row + 7, 0:n] * scale
        ng_ref[0:1, a0 : a0 + n] = fin[56 * t + 7 : 56 * t + 8, 0:n] * scale
        ng_ref[1:2, a0 : a0 + n] = fin[56 * t + 15 : 56 * t + 16, 0:n] * scale
    for i in range(HT):
        rp_ref[0:1, 128 * i : 128 * i + 128] = fin[336 + i : 337 + i, :] * scale
        rp_ref[1:2, 128 * i : 128 * i + 128] = fin[360 + i : 361 + i, :] * scale


def shards(
    act_codes, act_exponents, grad_codes, grad_exponents, conv_kernel, conv_bias,
    norm_gain, norm_shift, proj_in, proj_bias, response_gain, proj_out,
):
    vmem = pl.BlockSpec(memory_space=pltpu.VMEM)
    hbm = pl.BlockSpec(memory_space=pl.ANY)
    dma = pltpu.SemaphoreType.DMA
    scratch = [
        pltpu.VMEM((R, W, C), BF16),
        pltpu.VMEM((C // 32, R, W), jnp.int32),
        pltpu.VMEM((R, W, C), BF16),
        pltpu.VMEM((C // 32, R, W), jnp.int32),
        pltpu.VMEM((7, 7, C), F32),
        pltpu.VMEM((C,), F32),
        pltpu.VMEM((C,), F32),
        pltpu.VMEM((C,), F32),
        pltpu.VMEM((HT, 128), F32),
        pltpu.VMEM((HT, 128), F32),
        pltpu.VMEM((CP, H), BF16),
        pltpu.VMEM((CP, H), BF16),
        pltpu.VMEM((7, 8, CP), F32),
        pltpu.VMEM((8, CP), F32),
        pltpu.VMEM((R, W, CP), BF16),
        pltpu.VMEM((R, W, CP), BF16),
        pltpu.VMEM((R + 6, W, CP), BF16),
        pltpu.VMEM((R, W, CP), BF16),
        pltpu.VMEM((R + 6, W, CP), BF16),
        pltpu.VMEM((T, CP), F32),
        pltpu.VMEM((T, CP), F32),
        pltpu.VMEM((T, 128), F32),
        pltpu.VMEM((T, CP), BF16),
        pltpu.VMEM((8, T, CP), BF16),
        pltpu.VMEM((T, H), F32),
        pltpu.VMEM((T, H), F32),
        pltpu.VMEM((T, H), F32),
        pltpu.VMEM((T, H), BF16),
        pltpu.VMEM((H // 2, T), F32),
        pltpu.VMEM((2, 8, S // 2, T), BF16),
        pltpu.VMEM((2, S // 2, 8 * T), BF16),
        pltpu.VMEM((24, 128), F32),
        pltpu.VMEM((24, 128), F32),
        pltpu.VMEM((8, 24, 128), F32),
        pltpu.VMEM((8, 24, 128), F32),
        pltpu.VMEM((2, 24, 128), F32),
        pltpu.VMEM((2, S // 2 + 8, CP), F32),
        pltpu.VMEM((2, 4, 48, CP), F32),
        pltpu.VMEM((2, 4, 48, CP), BF16),
        pltpu.VMEM((2, 3, 48, CP), BF16),
        pltpu.VMEM((2, 56, CP), F32),
        pltpu.VMEM((8, 16, CP), BF16),
        pltpu.VMEM((T, CP), F32),
        pltpu.VMEM((R + 6, W, 128), F32),
        pltpu.VMEM((512, 128), F32),
        pltpu.VMEM((32, 16, 128), F32),
        pltpu.VMEM((16, 128), F32),
        pltpu.VMEM((8, 16, 128), F32),
        pltpu.VMEM((16, 128), F32),
        pltpu.VMEM((R, W, C), BF16),
        dma((2,)), dma((10,)),
        dma((4,)), dma((4,)),
        dma((8,)), dma((8,)),
        dma((2,)), dma((2,)),
        dma, dma,
        dma, dma,
        dma((2,)), dma((2,)),
        dma((2,)),
        dma((2,)), dma((2,)),
        dma, dma,
        dma, dma,
        dma,
        dma, dma,
        dma, dma,
        dma((1,)), dma((1,)),
    ]
    outs = pl.pallas_call(
        body,
        out_shape=(
            jax.ShapeDtypeStruct((R, W, C), BF16),
            jax.ShapeDtypeStruct((8, 16, CP), BF16),
            jax.ShapeDtypeStruct((512, 128), F32),
        ),
        in_specs=[hbm] * 12,
        out_specs=(hbm,) * 3,
        scratch_shapes=scratch,
        compiler_params=pltpu.CompilerParams(
            collective_id=0, has_side_effects=True, vmem_limit_bytes=56 * 1024 * 1024
        ),
    )(
        act_codes[0],
        act_exponents[0].transpose(2, 0, 1),
        grad_codes[0],
        grad_exponents[0].transpose(2, 0, 1),
        conv_kernel,
        conv_bias,
        norm_gain,
        norm_shift,
        proj_in.T,
        proj_bias.reshape(HT, 128),
        response_gain.reshape(HT, 128),
        proj_out.T,
    )
    results = pl.pallas_call(
        finish,
        out_shape=(
            jax.ShapeDtypeStruct((R, W, C), BF16),
            jax.ShapeDtypeStruct((U, C), F32),
            jax.ShapeDtypeStruct((7, 7, C), F32),
            jax.ShapeDtypeStruct((2, C), F32),
            jax.ShapeDtypeStruct((2, H), F32),
        ),
        in_specs=[vmem] * 3,
        out_specs=(vmem,) * 5,
    )(*outs)
    return (results[0][None],) + tuple(results[1:])


def solution(mesh):
    strips = P("dp", "rows", None, None)
    return jax.shard_map(
        shards,
        mesh=mesh,
        in_specs=(strips,) * 4 + (P(),) * 8,
        out_specs=(strips, P(("dp", "rows"), None), P(), P(), P()),
        check_vma=False,
    )
```

```python
import math

import jax
import jax.numpy as jnp
from jax import lax
from jax.experimental import pallas as pl
from jax.experimental.pallas import tpu as pltpu
from jax.sharding import PartitionSpec as P

NORM_EPSILON = 1e-06
RESPONSE_EPSILON = 1e-06
HALF_ROOT = 0.7071067811865476
NORMAL_PEAK = 0.3989422804014327

C = 704
CP = 768
CT = CP // 128
H = 2816
HT = H // 128
R = 4
W = 32
T = R * W
S = H // 8
B = S // 4
U = B // 8
F32 = jnp.float32
BF16 = jnp.bfloat16

ALPHA = (
    0.00022905065861350646,
    0.0034082910107109506,
    0.050955695062380861,
    0.18520832239976145,
    1.128379143519084,
)
BETA = (
    -1.1791602954361697e-7,
    0.000023547966471313185,
    0.0010179625278914885,
    0.014070470171167667,
    0.11098505178285362,
    0.49746925110067538,
    1.0,
)


def erf(v):
    v = jnp.clip(v, -3.7439211627767994, 3.7439211627767994)
    s = v * v
    top = jnp.full_like(s, ALPHA[0])
    for c in ALPHA[1:]:
        top = top * s + c
    low = jnp.full_like(s, BETA[0])
    for c in BETA[1:]:
        low = low * s + c
    return v * top / low


class Phases:
    def __init__(self):
        self.scope = None

    def __call__(self, name=None):
        if self.scope is not None:
            self.scope.__exit__(None, None, None)
        self.scope = jax.named_scope(name) if name else None
        if self.scope is not None:
            self.scope.__enter__()


class Post:
    def __init__(self):
        self.leaving, self.coming, self.inside = [], [], []

    @staticmethod
    def under(cond, f):
        if cond is None:
            f()
        else:
            pl.when(cond)(f)

    def send(self, copy, sends=None, receives=None, came=True):
        self.under(sends, copy.start)
        self.leaving.append((copy, sends))
        if came:
            self.coming.append((copy, receives))
        return copy

    def together(self, copies, whole, sends=None):
        sends = sends or [None] * len(copies)
        for copy, cond in zip(copies, sends, strict=True):
            self.under(cond, copy.start)
        if whole is not None:
            self.leaving.append((whole, None))
            self.coming.append((whole, None))
        return [whole]

    def partly(self, leaving, coming):
        self.leaving += leaving
        self.coming += coming
        return [whole for whole, _ in coming]

    def arrive(self, copies):
        for copy in copies:
            (entry,) = [e for e in self.coming if e[0] is copy]
            self.coming = [e for e in self.coming if e[0] is not copy]
            self.under(entry[1], copy.wait_recv)

    def left(self, copies):
        for copy in copies:
            (entry,) = [e for e in self.leaving if e[0] is copy]
            self.leaving = [e for e in self.leaving if e[0] is not copy]
            self.under(entry[1], copy.wait_send)

    def move(self, copy, cond=None):
        self.under(cond, copy.start)
        self.inside.append((copy, cond))
        return copy

    def moved(self, copies):
        for copy in copies:
            (entry,) = [e for e in self.inside if e[0] is copy]
            self.inside = [e for e in self.inside if e[0] is not copy]
            self.under(entry[1], copy.wait)

    def drain(self):
        self.moved([e[0] for e in self.inside])
        self.arrive([e[0] for e in self.coming])
        self.left([e[0] for e in self.leaving])


def lanes(i, n=128):
    return pl.ds(pl.multiple_of(i * n, n), n)


def moved(v, d):
    if d == 0:
        return v
    w = lax.broadcasted_iota(jnp.int32, v.shape, 0) + d
    return jnp.where((w >= 0) & (w < W), pltpu.roll(v, (-d) % W, 0), 0.0)


def depthwise(rows, weight):
    out = [None] * R
    for b in range(7):
        for r in range(R):
            acc = rows[r] * weight(0, b)
            for a in range(1, 7):
                acc = acc + rows[r + a] * weight(a, b)
            acc = moved(acc, b - 3)
            out[r] = acc if out[r] is None else out[r] + acc
    return out


def body(
    act_in, aexp_in, grad_in, gexp_in, ck_in, cb_in, gain_in, shift_in,
    win_hbm, pb_in, rg_in, wout_hbm,
    ig_ref, zr, fin,
    act_ref, aexp_ref, grad_ref, gexp_ref, ck_ref, cb_ref, gain_ref, shift_ref, pb_ref, rg_ref,
    win, wout, ckp, prm, sx, su, xs, up, mg, mx, normed, inv, ni, niall,
    act, gp, dg, pg, pgtf, pgt, pgr, stq, stp, rq, rp, coef, dwf, dwp, dwb, xr, zacc, zs,
    ngb, xf, red, redr, ysum, yr, zsum, zar, back, og,
    wsem, isem, ssend, srecv, hsend, hrecv, gsend, grecv, nsend, nrecv, fsend, frecv,
    psend, precv, lsem, xsend, xrecv, zsend, zrecv, rsend, rrecv, ysend, yrecv,
    zlocal, asend, arecv, qsend, qrecv, osend, orecv,
):
    phase = Phases()
    post = Post()
    phase("greet")
    dp, rw = lax.axis_index("dp"), lax.axis_index("rows")
    core = lax.rem(dp, 2)
    y = lax.rem(lax.div(dp, 2), 4)
    zl = lax.div(dp, 8)
    x = lax.div(rw, 2)
    zh = lax.rem(rw, 2)
    z = zh * 4 + zl
    gx = 2 * x + core
    gy = 2 * y + core

    def dev(x=x, y=y, zl=zl, zh=zh, core=core):
        return {"dp": (zl * 4 + y) * 2 + core, "rows": x * 2 + zh}

    def in_gx(i):
        m = lax.rem(gx + i, 8)
        return dev(x=lax.div(m, 2), core=lax.rem(m, 2))

    def in_gy(i):
        m = lax.rem(gy + i, 8)
        return dev(y=lax.div(m, 2), core=lax.rem(m, 2)), m

    def in_layer(iy, i):
        m, yy = lax.rem(gx + i, 8), lax.rem(y + iy, 4)
        return dev(x=lax.div(m, 2), core=lax.rem(m, 2), y=yy), m, yy

    layer = [(iy, i) for iy in range(4) for i in range(8)][1:]

    def in_z(i):
        m = lax.rem(z + i, 8)
        return dev(zl=lax.rem(m, 4), zh=lax.div(m, 4))

    swap = core != zh
    swap_dev = dev(zh=1 - zh, core=1 - core)
    sib = dev(core=1 - core)

    def remote(src, dst, send, recv, to):
        return pltpu.make_async_remote_copy(
            src_ref=src, dst_ref=dst, send_sem=send, recv_sem=recv,
            device_id=to, device_id_type=pl.DeviceIdType.MESH,
        )

    loads = [
        pltpu.make_async_copy(a, b, isem.at[k])
        for k, (a, b) in enumerate(
            (
                (aexp_in, aexp_ref), (act_in, act_ref), (gexp_in, gexp_ref), (grad_in, grad_ref),
                (ck_in, ck_ref), (cb_in, cb_ref), (gain_in, gain_ref), (shift_in, shift_ref),
                (pb_in, pb_ref), (rg_in, rg_ref),
            )
        )
    ]
    win_copy = pltpu.make_async_copy(win_hbm, win.at[pl.ds(0, C)], wsem.at[0])
    wout_copy = pltpu.make_async_copy(wout_hbm, wout.at[pl.ds(0, C)], wsem.at[1])

    for c in loads + [win_copy, wout_copy]:
        post.move(c)

    barrier = pltpu.get_barrier_semaphore()

    def greet(d):
        pl.semaphore_signal(
            barrier, inc=1, device_id=d, device_id_type=pl.DeviceIdType.MESH
        )

    @pl.when(swap)
    def _():
        greet(swap_dev)

    for iy, i in layer:
        greet(in_layer(iy, i)[0])
    for i in range(1, 8):
        greet(in_z(i))
    guests = 38 + jnp.where(swap, 1, 0)

    phase("scale")
    member = lax.broadcasted_iota(jnp.int32, (C // 32, CP), 1) // 32
    block = lax.broadcasted_iota(jnp.int32, (C // 32, CP), 0)
    spread = jnp.where(member == block, 1.0, 0.0).astype(BF16)

    def scaled(codes, exps, out):
        for r in range(R):
            power = jnp.exp2(exps[:, r, :].astype(F32)).astype(BF16)
            full = lax.dot_general(
                power, spread, (((0,), (0,)), ((), ())), preferred_element_type=F32
            )
            out[r, :, C - 64 : CP] = jnp.zeros((W, CP - C + 64), BF16)
            out[r, :, 0:C] = (codes[r].astype(F32) * full[:, 0:C]).astype(BF16)

    post.moved(loads[0:2])
    scaled(act_ref, aexp_ref, sx)

    phase("barrier")
    pl.semaphore_wait(barrier, guests)
    phase("scale2")

    thirds = [pl.ds(CP // 3 * k, CP // 3) for k in range(3)]
    swap_x = [
        remote(sx.at[:, :, at], xs.at[pl.ds(3, R), :, at], ssend.at[k], srecv.at[k], swap_dev)
        for k, at in enumerate(thirds)
    ]
    swap_u = remote(su, up, ssend.at[3], srecv.at[3], swap_dev)

    post.send(swap_x[0], swap, swap)
    post.moved(loads[2:])
    scaled(grad_ref, gexp_ref, su)

    @pl.when(jnp.logical_not(swap))
    def _():
        xs[3 : 3 + R] = sx[...]
        up[...] = su[...]

    ckp[...] = jnp.zeros_like(ckp)
    prm[...] = jnp.zeros_like(prm)
    ckp[:, 0:7, 0:C] = ck_ref[...]
    prm[0:1, 0:C] = cb_ref[...].reshape(1, C)
    prm[1:2, 0:C] = gain_ref[...].reshape(1, C)
    prm[2:3, 0:C] = shift_ref[...].reshape(1, C)
    win[C:CP, :] = jnp.zeros((CP - C, H), BF16)
    wout[C:CP, :] = jnp.zeros((CP - C, H), BF16)
    first, last = gx == 0, gx == 7

    @pl.when(first)
    def _():
        xs[0:3] = jnp.zeros((3, W, CP), BF16)
        mg[0:3] = jnp.zeros((3, W, CP), BF16)

    @pl.when(last)
    def _():
        xs[7:10] = jnp.zeros((3, W, CP), BF16)
        mg[7:10] = jnp.zeros((3, W, CP), BF16)

    below, above = lax.rem(gx + 1, 8), lax.rem(gx + 7, 8)
    below_dev = dev(x=lax.div(below, 2), core=lax.rem(below, 2))
    above_dev = dev(x=lax.div(above, 2), core=lax.rem(above, 2))

    def halo(buf, base, at=slice(None)):
        down = remote(buf.at[pl.ds(4, 3), :, at], buf.at[pl.ds(0, 3), :, at],
                      hsend.at[base], hrecv.at[base], below_dev)
        upward = remote(buf.at[pl.ds(3, 3), :, at], buf.at[pl.ds(7, 3), :, at],
                        hsend.at[base + 1], hrecv.at[base + 1], above_dev)

        post.send(down, jnp.logical_not(last), jnp.logical_not(first))
        post.send(upward, jnp.logical_not(first), jnp.logical_not(last))
        return [down, upward]

    def conv_tile(t, _):
        at = lanes(t)
        rows = [xs[i, :, at].astype(F32) for i in range(R + 6)]
        out = depthwise(rows, lambda a, b: ckp[a, b : b + 1, at])
        for r in range(R):
            mx[pl.ds(r * W, W), at] = out[r] + prm[0:1, at]
        return 0

    near = []
    for k in range(4):
        if k < 3:
            phase("swap_wait%d" % k)
            post.left([swap_x[k]])
            if k < 2:
                post.send(swap_x[k + 1], swap, swap)
            else:
                post.send(swap_u, swap, swap)
            post.arrive([swap_x[k]])
            near.append(halo(xs, 2 * k, thirds[k]))
        if k > 0:
            phase("halo_wait%d" % (k - 1))
            post.arrive(near[k - 1])
            phase("conv%d" % (k - 1))
            lax.fori_loop((k - 1) * CT // 3, k * CT // 3, conv_tile, 0)
    phase("norm")
    inside = lax.broadcasted_iota(jnp.int32, (W, CP), 1) < C

    def norm_block(r, _):
        at = pl.ds(pl.multiple_of(r * W, W), W)
        v = mx[at, :]
        centered = jnp.where(inside, v - jnp.sum(v, axis=1, keepdims=True) / C, 0.0)
        var = jnp.sum(centered * centered, axis=1, keepdims=True) / C
        inverse = lax.rsqrt(var + NORM_EPSILON)
        n = centered * inverse
        normed[at, :] = n
        inv[at, :] = jnp.broadcast_to(inverse, (W, 128))
        ni[at, :] = (n * prm[1:2, :] + prm[2:3, :]).astype(BF16)
        return 0

    lax.fori_loop(0, R, norm_block, 0)

    three = niall.at[pl.ds(0, 3)]
    ni_copies = post.together(
        [
            remote(ni, niall.at[gy], nsend, nrecv, dev(y=lax.rem(y + i, 4)))
            for i in range(1, 4)
        ],
        remote(three, three, nsend, nrecv, sib),
    )
    niall[gy] = ni[...]

    phase("win_wait")
    stq[...] = jnp.zeros_like(stq)
    stp[...] = jnp.zeros_like(stp)
    red[...] = jnp.zeros_like(red)
    post.moved([win_copy])
    phase("active")

    def active(i, _):
        at = lanes(i, 256)
        bias = [pb_ref[pl.ds(2 * i + k, 1), :] for k in range(2)]
        p = jnp.dot(ni[...], win[:, at], preferred_element_type=F32)
        p = p + jnp.concatenate(bias, axis=1)
        phi = 0.5 * (1.0 + erf(p * HALF_ROOT))
        v = p * phi
        act[:, at] = v
        gp[:, at] = phi + p * (NORMAL_PEAK * jnp.exp(-0.5 * p * p))
        s = jnp.sum(v * v, axis=0, keepdims=True)
        stq[pl.ds(2 * i, 1), :] = s[:, 0:128]
        stq[pl.ds(2 * i + 1, 1), :] = s[:, 128:256]
        return 0

    lax.fori_loop(0, HT // 2, active, 0, unroll=True)

    def to_group(src, dst, send, recv):
        seven = dst.at[pl.ds(0, 7)]
        return post.together(
            [remote(src, dst.at[gx], send, recv, in_gx(i)) for i in range(1, 8)],
            remote(seven, seven, send, recv, sib),
        )

    q_copies = to_group(stq, rq, gsend.at[0], grecv.at[0])
    rq[gx] = stq[...]

    phase("up_wait")
    post.arrive([swap_u])
    post.moved([wout_copy])
    phase("down")
    uf = up[...].reshape(T, CP)

    dg[...] = jnp.dot(uf, wout[...], preferred_element_type=F32)

    def downward(i, _):
        at = lanes(i, 256)
        d = dg[:, at]
        s = jnp.sum(d * act[:, at], axis=0, keepdims=True)
        stp[pl.ds(2 * i, 1), :] = s[:, 0:128]
        stp[pl.ds(2 * i + 1, 1), :] = s[:, 128:256]
        e = jnp.sum(d, axis=0, keepdims=True)
        red[pl.ds(360 + 2 * i, 1), :] = e[:, 0:128]
        red[pl.ds(361 + 2 * i, 1), :] = e[:, 128:256]
        return 0

    lax.fori_loop(0, HT // 2, downward, 0, unroll=True)
    p_copies = to_group(stp, rp, gsend.at[1], grecv.at[1])
    rp[gx] = stp[...]

    phase("response")
    post.arrive(q_copies)
    squares = rq[0, 0:HT]
    for i in range(1, 8):
        squares = squares + rq[i, 0:HT]
    magnitude = jnp.sqrt(squares + RESPONSE_EPSILON)
    denominator = jnp.sum(magnitude) / H + RESPONSE_EPSILON
    response = magnitude / denominator
    coef[0, 0:HT] = 1.0 + rg_ref[...] * response
    red[336 : 336 + HT] = response * stp[0:HT]
    post.arrive(p_copies)
    products = rp[0, 0:HT]
    for i in range(1, 8):
        products = products + rp[i, 0:HT]
    scaled_products = rg_ref[...] * products
    magnitude_grad = scaled_products / denominator - jnp.sum(
        scaled_products * magnitude
    ) / (denominator * denominator * H)
    coef[1, 0:HT] = magnitude_grad / magnitude

    phase("preact")
    own = pl.ds(pl.multiple_of(gy * 128, 128), 128)
    a_copies = [[], []]

    def exchange(h):
        copies = []
        for i in range(1, 8):
            to, m = in_gy(i)
            copies.append(
                remote(pgt.at[h, m], pgr.at[h, :, own], psend.at[h], precv.at[h], to)
            )
        seven = pgt.at[h, pl.ds(0, 7)]
        a_copies[h] = post.together(
            copies, remote(seven, seven, psend.at[h], precv.at[h], sib)
        )

    def backward(h):
        at = pl.ds(h * (H // 2), H // 2)
        return lax.dot_general(
            pg[:, at], win[:, at], (((1,), (1,)), ((), ())), preferred_element_type=F32
        )

    for h in range(2):

        def preact(i, _):
            j = h * (HT // 2) + i
            at = lanes(j)
            a = coef[0, pl.ds(j, 1), :]
            b = coef[1, pl.ds(j, 1), :]
            g = (dg[:, at] * a + act[:, at] * b) * gp[:, at]
            pg[:, at] = g.astype(BF16)
            turned = g.T
            for k in range(16):
                n = i * 16 + k
                q = lax.div(n, B // 8)
                to = (lax.rem(q, 8) * 2 + lax.div(q, 8)) * B + lax.rem(n, B // 8) * 8
                pgtf[pl.ds(pl.multiple_of(to, 8), 8), :] = turned[8 * k : 8 * k + 8, :]
            return 0

        lax.fori_loop(0, HT // 2, preact, 0, unroll=True)
        pgt[h] = pgtf[...].astype(BF16).reshape(8, S // 2, T)
        pgr[h, :, own] = pgt[h, gy]
        if h == 0:
            exchange(0)
            ngb[...] = backward(0)

    phase("normed_grad")
    ngb[...] = ngb[...] + backward(1)
    exchange(1)
    phase("norm_grad")

    def norm_grad(r, sums):
        at = pl.ds(pl.multiple_of(r * W, W), W)
        g = ngb[at, :]
        n = normed[at, :]
        gn = g * n
        s = g * prm[1:2, :]
        m1 = jnp.sum(s, axis=1, keepdims=True) / C
        m2 = jnp.sum(s * n, axis=1, keepdims=True) / C
        v = inv[at, :][:, 0:1] * (s - m1 - n * m2)
        mg[3 + r] = jnp.where(inside, v, 0.0).astype(BF16)
        return (
            sums[0] + jnp.sum(gn, axis=0, keepdims=True),
            sums[1] + jnp.sum(g, axis=0, keepdims=True),
        )

    zero = jnp.zeros((1, CP), F32)
    gain_part, shift_part = lax.fori_loop(0, R, norm_grad, (zero, zero))
    m_copies = halo(mg, 6)

    phase("kernel_grad")
    def kernel_tile(t, _):
        at = lanes(t)
        for i in range(R + 6):
            xf[i] = xs[i, :, at].astype(F32)
        g = [mg[3 + r, :, at].astype(F32) for r in range(R)]
        base = t * 56
        for b in range(7):
            gs = [moved(v, 3 - b) for v in g]
            for a in range(7):
                s = xf[a] * gs[0]
                for r in range(1, R):
                    s = s + xf[a + r] * gs[r]
                red[pl.ds(base + a * 8 + b, 1), :] = jnp.sum(s, axis=0, keepdims=True)
        return 0

    for t in range(CT):
        red[56 * t + 7 : 56 * t + 8, :] = gain_part[:, 128 * t : 128 * t + 128]
        red[56 * t + 15 : 56 * t + 16, :] = shift_part[:, 128 * t : 128 * t + 128]

    def share(m):
        return pl.ds(pl.multiple_of(m * 64, 8), 64)

    adds = gx < 6
    rest = jnp.logical_not(adds)

    def scatter(low, high):
        for i in range(1, 8):
            m = lax.rem(gx + i, 8)
            copy = remote(red.at[share(m)], redr.at[gx], rsend, rrecv, in_gx(i))
            pl.when((m >= low) & (m < high))(copy.start)

    lax.fori_loop(0, 4, kernel_tile, 0)
    scatter(0, 3)
    lax.fori_loop(4, CT, kernel_tile, 0)
    scatter(3, 6)
    sizes = [redr.at[pl.ds(0, k)] for k in (5, 6, 7)]
    five, six, seven = [remote(v, v, rsend, rrecv, sib) for v in sizes]
    r_copies = post.partly([(five, adds), (six, rest)], [(seven, adds)])

    @pl.when(adds)
    def _():
        redr[gx] = red[share(gx), :]

    phase("ni_wait")
    post.arrive(ni_copies)
    pieces = [niall.at[2 * k + core] for k in range(4)]
    four = niall.at[pl.ds(0, 4)]
    f_copies = post.together(
        [remote(p, p, fsend, frecv, sib) for p in pieces],
        remote(four, four, fsend, frecv, sib),
    )

    x_copies = [[], []]

    def weight(h):
        phase("pgr_wait%d" % h)
        post.arrive(a_copies[h])
        if h == 0:
            post.arrive(f_copies)
        phase("dw%d" % h)
        dwf[h, S // 2 :, :] = jnp.zeros((8, CP), F32)
        dwf[h, 0 : S // 2, :] = jnp.dot(
            pgr[h], niall[...].reshape(8 * T, CP), preferred_element_type=F32
        )
        for k in range(4):
            part = jnp.concatenate(
                [dwf[h, B * e + 2 * U * k : B * e + 2 * U * k + 24, :] for e in range(2)]
            )
            dwp[h, k] = part
            dwb[h, k] = part.astype(BF16)
        copies = []
        for i in range(1, 4):
            k = lax.rem(x + i, 4)
            copies.append(
                remote(dwb.at[h, k], xr.at[h, i - 1], xsend.at[h], xrecv.at[h], dev(x=k))
            )
        x_copies[h] = post.together(
            copies, remote(xr.at[h], xr.at[h], xsend.at[h], xrecv.at[h], sib)
        )

    def shares(h):
        phase("x_wait%d" % h)
        post.arrive(x_copies[h])
        phase("z_send%d" % h)
        zacc[h, 48:56, :] = jnp.zeros((8, CP), F32)
        total = dwp[h, x]
        for i in range(3):
            total = total + xr[h, i].astype(F32)
        zacc[h, 0:48, :] = total
        for e in range(2):
            for hi in range(2):
                g = (h * 2 + e) * 2 + hi
                zs[g] = zacc[h, 24 * e + U * hi : 24 * e + U * hi + 16, :].astype(BF16)
                to = hi * 4 + h * 2 + e
                copy = remote(
                    zs.at[g], zr.at[z], zsend, zrecv,
                    dev(zl=jnp.int32(h * 2 + e), zh=jnp.int32(hi)),
                )
                post.together([copy], None, [z != to])
                own_share = pltpu.make_async_copy(zs.at[g], zr.at[z], zlocal)
                pl.when(z == to)(own_share.start)

    weight(0)

    phase("m_wait")
    post.arrive(m_copies)
    phase("back")

    def back_tile(t, _):
        at = lanes(t)
        rows = [mg[i, :, at].astype(F32) for i in range(R + 6)]
        out = depthwise(rows, lambda a, b: ckp[6 - a, 6 - b : 7 - b, at])
        for r in range(R):
            sx[r, :, at] = (out[r] + up[r, :, at].astype(F32)).astype(BF16)
        return 0

    o_copies, o_locals = [], []
    for k in range(3):
        lax.fori_loop(k * CT // 3, (k + 1) * CT // 3, back_tile, 0)
        n = min(256, C - 256 * k)
        at = pl.ds(256 * k, n)
        og[:, :, 256 * k : 256 * k + n] = sx[:, :, 256 * k : 256 * k + n]
        src, dst = og.at[:, :, at], ig_ref.at[:, :, at]
        copy = remote(src, dst, osend.at[k], orecv.at[k], swap_dev)
        o_copies.append(post.send(copy, swap, swap))
        copy = pltpu.make_async_copy(src, dst, lsem.at[2 + k])
        o_locals.append(post.move(copy, jnp.logical_not(swap)))

    phase("r_wait")
    post.arrive(r_copies)
    three = remote(yr.at[pl.ds(0, 3)], yr.at[pl.ds(0, 3)], ysend, yrecv, sib)
    y_copies = post.partly([(three, adds)], [(three, adds)])

    @pl.when(adds)
    def _():
        total = redr[0]
        for i in range(1, 8):
            total = total + redr[i]
        ysum[...] = total.reshape(4, 16, 128)
        for i in range(1, 4):
            k = lax.rem(y + i, 4)
            remote(ysum.at[k], yr.at[y], ysend, yrecv, dev(y=k)).start()
        yr[y] = ysum[y]

    weight(1)
    phase("y_wait")
    post.arrive(y_copies)
    seven = remote(zar.at[pl.ds(0, 7)], zar.at[pl.ds(0, 7)], asend, arecv, sib)
    s_copies = post.partly([(seven, adds)], [(seven, adds)])

    @pl.when(adds)
    def _():
        zsum[...] = yr[0] + yr[1] + yr[2] + yr[3]
        for i in range(1, 8):
            remote(zsum, zar.at[z], asend, arecv, in_z(i)).start()
        zar[z] = zsum[...]

    shares(0)
    shares(1)

    phase("s_wait")
    post.arrive(s_copies)
    mine = pl.ds(pl.multiple_of(gx * 64 + y * 16, 8), 16)
    sizes = [red.at[pl.ds(0, 16 * k)] for k in (31, 23, 24)]
    sent, more, all_of = [remote(v, v, qsend, qrecv, sib) for v in sizes]
    l_copies = post.partly([(sent, adds)], [(more, adds), (all_of, rest)])
    own_sums = pltpu.make_async_copy(back, fin.at[mine], lsem.at[1])

    @pl.when(adds)
    def _():
        total = zar[0]
        for i in range(1, 8):
            total = total + zar[i]
        back[...] = total
        for iy, i in layer:
            remote(back, fin.at[mine], qsend, qrecv, in_layer(iy, i)[0]).start()
        own_sums.start()

    post.inside.append((own_sums, adds))
    seven = zs.at[pl.ds(0, 7)]
    z_comes = post.together([], remote(seven, seven, zsend, zrecv, sib))
    phase("z_wait")
    post.arrive(z_comes)
    phase("l_wait")
    post.arrive(l_copies)
    phase("o_wait")
    post.arrive(o_copies)
    post.moved(o_locals + [own_sums])
    pltpu.make_async_copy(zs.at[0], zr.at[z], zlocal).wait()

    phase("sends")
    post.drain()
    phase()


def finish(ig_ref, zr, fin, out_ref, dw_ref, kg_ref, ng_ref, rp_ref):
    out_ref[...] = ig_ref[...]
    scale = 1.0 / math.sqrt(32.0 * 32.0 * 32.0)
    total = zr[0].astype(F32)
    for k in range(1, 8):
        total = total + zr[k].astype(F32)
    dw_ref[...] = total[0:U, 0:C] * scale
    for t in range(CT):
        a0, n = 128 * t, min(128, C - 128 * t)
        for a in range(7):
            row = 56 * t + 8 * a
            kg_ref[a, :, a0 : a0 + n] = fin[row : row + 7, 0:n] * scale
        ng_ref[0:1, a0 : a0 + n] = fin[56 * t + 7 : 56 * t + 8, 0:n] * scale
        ng_ref[1:2, a0 : a0 + n] = fin[56 * t + 15 : 56 * t + 16, 0:n] * scale
    for i in range(HT):
        rp_ref[0:1, 128 * i : 128 * i + 128] = fin[336 + i : 337 + i, :] * scale
        rp_ref[1:2, 128 * i : 128 * i + 128] = fin[360 + i : 361 + i, :] * scale


def shards(
    act_codes, act_exponents, grad_codes, grad_exponents, conv_kernel, conv_bias,
    norm_gain, norm_shift, proj_in, proj_bias, response_gain, proj_out,
):
    vmem = pl.BlockSpec(memory_space=pltpu.VMEM)
    hbm = pl.BlockSpec(memory_space=pl.ANY)
    dma = pltpu.SemaphoreType.DMA
    scratch = [
        pltpu.VMEM((R, W, C), BF16),
        pltpu.VMEM((C // 32, R, W), jnp.int32),
        pltpu.VMEM((R, W, C), BF16),
        pltpu.VMEM((C // 32, R, W), jnp.int32),
        pltpu.VMEM((7, 7, C), F32),
        pltpu.VMEM((C,), F32),
        pltpu.VMEM((C,), F32),
        pltpu.VMEM((C,), F32),
        pltpu.VMEM((HT, 128), F32),
        pltpu.VMEM((HT, 128), F32),
        pltpu.VMEM((CP, H), BF16),
        pltpu.VMEM((CP, H), BF16),
        pltpu.VMEM((7, 8, CP), F32),
        pltpu.VMEM((8, CP), F32),
        pltpu.VMEM((R, W, CP), BF16),
        pltpu.VMEM((R, W, CP), BF16),
        pltpu.VMEM((R + 6, W, CP), BF16),
        pltpu.VMEM((R, W, CP), BF16),
        pltpu.VMEM((R + 6, W, CP), BF16),
        pltpu.VMEM((T, CP), F32),
        pltpu.VMEM((T, CP), F32),
        pltpu.VMEM((T, 128), F32),
        pltpu.VMEM((T, CP), BF16),
        pltpu.VMEM((8, T, CP), BF16),
        pltpu.VMEM((T, H), F32),
        pltpu.VMEM((T, H), F32),
        pltpu.VMEM((T, H), F32),
        pltpu.VMEM((T, H), BF16),
        pltpu.VMEM((H // 2, T), F32),
        pltpu.VMEM((2, 8, S // 2, T), BF16),
        pltpu.VMEM((2, S // 2, 8 * T), BF16),
        pltpu.VMEM((24, 128), F32),
        pltpu.VMEM((24, 128), F32),
        pltpu.VMEM((8, 24, 128), F32),
        pltpu.VMEM((8, 24, 128), F32),
        pltpu.VMEM((2, 24, 128), F32),
        pltpu.VMEM((2, S // 2 + 8, CP), F32),
        pltpu.VMEM((2, 4, 48, CP), F32),
        pltpu.VMEM((2, 4, 48, CP), BF16),
        pltpu.VMEM((2, 3, 48, CP), BF16),
        pltpu.VMEM((2, 56, CP), F32),
        pltpu.VMEM((8, 16, CP), BF16),
        pltpu.VMEM((T, CP), F32),
        pltpu.VMEM((R + 6, W, 128), F32),
        pltpu.VMEM((512, 128), F32),
        pltpu.VMEM((8, 64, 128), F32),
        pltpu.VMEM((4, 16, 128), F32),
        pltpu.VMEM((4, 16, 128), F32),
        pltpu.VMEM((16, 128), F32),
        pltpu.VMEM((8, 16, 128), F32),
        pltpu.VMEM((16, 128), F32),
        pltpu.VMEM((R, W, C), BF16),
        dma((2,)), dma((10,)),
        dma((4,)), dma((4,)),
        dma((8,)), dma((8,)),
        dma((2,)), dma((2,)),
        dma, dma,
        dma, dma,
        dma((2,)), dma((2,)),
        dma((5,)),
        dma((2,)), dma((2,)),
        dma, dma,
        dma, dma,
        dma, dma,
        dma,
        dma, dma,
        dma, dma,
        dma((3,)), dma((3,)),
    ]
    outs = pl.pallas_call(
        body,
        out_shape=(
            jax.ShapeDtypeStruct((R, W, C), BF16),
            jax.ShapeDtypeStruct((8, 16, CP), BF16),
            jax.ShapeDtypeStruct((512, 128), F32),
        ),
        in_specs=[hbm] * 12,
        out_specs=(hbm,) * 3,
        scratch_shapes=scratch,
        compiler_params=pltpu.CompilerParams(
            collective_id=0, has_side_effects=True, vmem_limit_bytes=56 * 1024 * 1024
        ),
    )(
        act_codes[0],
        act_exponents[0].transpose(2, 0, 1),
        grad_codes[0],
        grad_exponents[0].transpose(2, 0, 1),
        conv_kernel,
        conv_bias,
        norm_gain,
        norm_shift,
        proj_in.T,
        proj_bias.reshape(HT, 128),
        response_gain.reshape(HT, 128),
        proj_out.T,
    )
    results = pl.pallas_call(
        finish,
        out_shape=(
            jax.ShapeDtypeStruct((R, W, C), BF16),
            jax.ShapeDtypeStruct((U, C), F32),
            jax.ShapeDtypeStruct((7, 7, C), F32),
            jax.ShapeDtypeStruct((2, C), F32),
            jax.ShapeDtypeStruct((2, H), F32),
        ),
        in_specs=[vmem] * 3,
        out_specs=(vmem,) * 5,
    )(*outs)
    return (results[0][None],) + tuple(results[1:])


def solution(mesh):
    strips = P("dp", "rows", None, None)
    return jax.shard_map(
        shards,
        mesh=mesh,
        in_specs=(strips,) * 4 + (P(),) * 8,
        out_specs=(strips, P(("dp", "rows"), None), P(), P(), P()),
        check_vma=False,
    )
```

```python
import math

import jax
import jax.numpy as jnp
from jax import lax
from jax.experimental import pallas as pl
from jax.experimental.pallas import tpu as pltpu
from jax.sharding import PartitionSpec as P

NORM_EPSILON = 1e-06
RESPONSE_EPSILON = 1e-06
HALF_ROOT = 0.7071067811865476
NORMAL_PEAK = 0.3989422804014327

C = 704
CP = 768
CT = CP // 128
H = 2816
HT = H // 128
R = 4
W = 32
T = R * W
S = H // 8
B = S // 4
U = B // 8
F32 = jnp.float32
BF16 = jnp.bfloat16

ALPHA = (
    0.00022905065861350646,
    0.0034082910107109506,
    0.050955695062380861,
    0.18520832239976145,
    1.128379143519084,
)
BETA = (
    -1.1791602954361697e-7,
    0.000023547966471313185,
    0.0010179625278914885,
    0.014070470171167667,
    0.11098505178285362,
    0.49746925110067538,
    1.0,
)


def erf(v):
    v = jnp.clip(v, -3.7439211627767994, 3.7439211627767994)
    s = v * v
    top = jnp.full_like(s, ALPHA[0])
    for c in ALPHA[1:]:
        top = top * s + c
    low = jnp.full_like(s, BETA[0])
    for c in BETA[1:]:
        low = low * s + c
    return v * top / low


class Phases:
    def __init__(self):
        self.scope = None

    def __call__(self, name=None):
        if self.scope is not None:
            self.scope.__exit__(None, None, None)
        self.scope = jax.named_scope(name) if name else None
        if self.scope is not None:
            self.scope.__enter__()


class Post:
    def __init__(self):
        self.leaving, self.coming, self.inside = [], [], []

    @staticmethod
    def under(cond, f):
        if cond is None:
            f()
        else:
            pl.when(cond)(f)

    def send(self, copy, sends=None, receives=None, came=True):
        self.under(sends, copy.start)
        self.leaving.append((copy, sends))
        if came:
            self.coming.append((copy, receives))
        return copy

    def together(self, copies, whole, sends=None):
        sends = sends or [None] * len(copies)
        for copy, cond in zip(copies, sends, strict=True):
            self.under(cond, copy.start)
        if whole is not None:
            self.leaving.append((whole, None))
            self.coming.append((whole, None))
        return [whole]

    def partly(self, leaving, coming):
        self.leaving += leaving
        self.coming += coming
        return [whole for whole, _ in coming]

    def arrive(self, copies):
        for copy in copies:
            (entry,) = [e for e in self.coming if e[0] is copy]
            self.coming = [e for e in self.coming if e[0] is not copy]
            self.under(entry[1], copy.wait_recv)

    def left(self, copies):
        for copy in copies:
            (entry,) = [e for e in self.leaving if e[0] is copy]
            self.leaving = [e for e in self.leaving if e[0] is not copy]
            self.under(entry[1], copy.wait_send)

    def move(self, copy, cond=None):
        self.under(cond, copy.start)
        self.inside.append((copy, cond))
        return copy

    def moved(self, copies):
        for copy in copies:
            (entry,) = [e for e in self.inside if e[0] is copy]
            self.inside = [e for e in self.inside if e[0] is not copy]
            self.under(entry[1], copy.wait)

    def drain(self):
        self.moved([e[0] for e in self.inside])
        self.arrive([e[0] for e in self.coming])
        self.left([e[0] for e in self.leaving])


def lanes(i, n=128):
    return pl.ds(pl.multiple_of(i * n, n), n)


def moved(v, d):
    if d == 0:
        return v
    w = lax.broadcasted_iota(jnp.int32, v.shape, 0) + d
    return jnp.where((w >= 0) & (w < W), pltpu.roll(v, (-d) % W, 0), 0.0)


def depthwise(rows, weight):
    out = [None] * R
    for b in range(7):
        for r in range(R):
            acc = rows[r] * weight(0, b)
            for a in range(1, 7):
                acc = acc + rows[r + a] * weight(a, b)
            acc = moved(acc, b - 3)
            out[r] = acc if out[r] is None else out[r] + acc
    return out


def body(
    act_in, aexp_in, grad_in, gexp_in, ck_in, cb_in, gain_in, shift_in,
    win_hbm, pb_in, rg_in, wout_hbm,
    ig_ref, zr, fin,
    act_ref, aexp_ref, grad_ref, gexp_ref, ck_ref, cb_ref, gain_ref, shift_ref, pb_ref, rg_ref,
    win, wout, ckp, prm, sx, su, xs, up, mg, mx, normed, inv, ni, niall,
    act, gp, dg, pg, pgtf, pgt, pgr, stq, stp, rq, rp, coef, dwf, dwp, dwb, xr, zacc, zs,
    ngb, xf, red, redr, ysum, yr, zsum, zar, back, og,
    wsem, isem, ssend, srecv, hsend, hrecv, gsend, grecv, nsend, nrecv, fsend, frecv,
    psend, precv, lsem, xsend, xrecv, zsend, zrecv, rsend, rrecv, ysend, yrecv,
    zlocal, asend, arecv, qsend, qrecv, osend, orecv,
):
    phase = Phases()
    post = Post()
    phase("greet")
    dp, rw = lax.axis_index("dp"), lax.axis_index("rows")
    core = lax.rem(dp, 2)
    y = lax.rem(lax.div(dp, 2), 4)
    zl = lax.div(dp, 8)
    x = lax.div(rw, 2)
    zh = lax.rem(rw, 2)
    z = zh * 4 + zl
    gx = 2 * x + core
    gy = 2 * y + core

    def dev(x=x, y=y, zl=zl, zh=zh, core=core):
        return {"dp": (zl * 4 + y) * 2 + core, "rows": x * 2 + zh}

    def in_gx(i):
        m = lax.rem(gx + i, 8)
        return dev(x=lax.div(m, 2), core=lax.rem(m, 2))

    def in_gy(i):
        m = lax.rem(gy + i, 8)
        return dev(y=lax.div(m, 2), core=lax.rem(m, 2)), m

    def in_layer(iy, i):
        m, yy = lax.rem(gx + i, 8), lax.rem(y + iy, 4)
        return dev(x=lax.div(m, 2), core=lax.rem(m, 2), y=yy), m, yy

    layer = [(iy, i) for iy in range(4) for i in range(8)][1:]

    def in_z(i):
        m = lax.rem(z + i, 8)
        return dev(zl=lax.rem(m, 4), zh=lax.div(m, 4))

    swap = core != zh
    swap_dev = dev(zh=1 - zh, core=1 - core)
    sib = dev(core=1 - core)

    def remote(src, dst, send, recv, to):
        return pltpu.make_async_remote_copy(
            src_ref=src, dst_ref=dst, send_sem=send, recv_sem=recv,
            device_id=to, device_id_type=pl.DeviceIdType.MESH,
        )

    loads = [
        pltpu.make_async_copy(a, b, isem.at[k])
        for k, (a, b) in enumerate(
            (
                (aexp_in, aexp_ref), (act_in, act_ref), (gexp_in, gexp_ref), (grad_in, grad_ref),
                (ck_in, ck_ref), (cb_in, cb_ref), (gain_in, gain_ref), (shift_in, shift_ref),
                (pb_in, pb_ref), (rg_in, rg_ref),
            )
        )
    ]
    win_copy = pltpu.make_async_copy(win_hbm, win.at[pl.ds(0, C)], wsem.at[0])
    wout_copy = pltpu.make_async_copy(wout_hbm, wout.at[pl.ds(0, C)], wsem.at[1])

    for c in loads + [win_copy, wout_copy]:
        post.move(c)

    barrier = pltpu.get_barrier_semaphore()

    def greet(d):
        pl.semaphore_signal(
            barrier, inc=1, device_id=d, device_id_type=pl.DeviceIdType.MESH
        )

    @pl.when(swap)
    def _():
        greet(swap_dev)

    for iy, i in layer:
        greet(in_layer(iy, i)[0])
    for i in range(1, 8):
        greet(in_z(i))
    guests = 38 + jnp.where(swap, 1, 0)

    phase("scale")
    member = lax.broadcasted_iota(jnp.int32, (C // 32, CP), 1) // 32
    block = lax.broadcasted_iota(jnp.int32, (C // 32, CP), 0)
    spread = jnp.where(member == block, 1.0, 0.0).astype(BF16)

    def scaled(codes, exps, out):
        for r in range(R):
            power = jnp.exp2(exps[:, r, :].astype(F32)).astype(BF16)
            full = lax.dot_general(
                power, spread, (((0,), (0,)), ((), ())), preferred_element_type=F32
            )
            out[r, :, C - 64 : CP] = jnp.zeros((W, CP - C + 64), BF16)
            out[r, :, 0:C] = (codes[r].astype(F32) * full[:, 0:C]).astype(BF16)

    post.moved(loads[0:2])
    scaled(act_ref, aexp_ref, sx)

    phase("barrier")
    pl.semaphore_wait(barrier, guests)
    phase("scale2")

    thirds = [pl.ds(CP // 3 * k, CP // 3) for k in range(3)]
    swap_x = [
        remote(sx.at[:, :, at], xs.at[pl.ds(3, R), :, at], ssend.at[k], srecv.at[k], swap_dev)
        for k, at in enumerate(thirds)
    ]
    swap_u = remote(su, up, ssend.at[3], srecv.at[3], swap_dev)

    for c in swap_x:
        post.send(c, swap, swap)
    post.moved(loads[2:])
    scaled(grad_ref, gexp_ref, su)

    @pl.when(jnp.logical_not(swap))
    def _():
        xs[3 : 3 + R] = sx[...]
        up[...] = su[...]

    ckp[...] = jnp.zeros_like(ckp)
    prm[...] = jnp.zeros_like(prm)
    ckp[:, 0:7, 0:C] = ck_ref[...]
    prm[0:1, 0:C] = cb_ref[...].reshape(1, C)
    prm[1:2, 0:C] = gain_ref[...].reshape(1, C)
    prm[2:3, 0:C] = shift_ref[...].reshape(1, C)
    win[C:CP, :] = jnp.zeros((CP - C, H), BF16)
    wout[C:CP, :] = jnp.zeros((CP - C, H), BF16)
    first, last = gx == 0, gx == 7

    @pl.when(first)
    def _():
        xs[0:3] = jnp.zeros((3, W, CP), BF16)
        mg[0:3] = jnp.zeros((3, W, CP), BF16)

    @pl.when(last)
    def _():
        xs[7:10] = jnp.zeros((3, W, CP), BF16)
        mg[7:10] = jnp.zeros((3, W, CP), BF16)

    below, above = lax.rem(gx + 1, 8), lax.rem(gx + 7, 8)
    below_dev = dev(x=lax.div(below, 2), core=lax.rem(below, 2))
    above_dev = dev(x=lax.div(above, 2), core=lax.rem(above, 2))

    def halo(buf, base, at=slice(None)):
        down = remote(buf.at[pl.ds(4, 3), :, at], buf.at[pl.ds(0, 3), :, at],
                      hsend.at[base], hrecv.at[base], below_dev)
        upward = remote(buf.at[pl.ds(3, 3), :, at], buf.at[pl.ds(7, 3), :, at],
                        hsend.at[base + 1], hrecv.at[base + 1], above_dev)

        post.send(down, jnp.logical_not(last), jnp.logical_not(first))
        post.send(upward, jnp.logical_not(first), jnp.logical_not(last))
        return [down, upward]

    def conv_tile(t, _):
        at = lanes(t)
        rows = [xs[i, :, at].astype(F32) for i in range(R + 6)]
        out = depthwise(rows, lambda a, b: ckp[a, b : b + 1, at])
        for r in range(R):
            mx[pl.ds(r * W, W), at] = out[r] + prm[0:1, at]
        return 0

    near = []
    for k in range(4):
        if k < 3:
            phase("swap_wait%d" % k)
            post.arrive([swap_x[k]])
            near.append(halo(xs, 2 * k, thirds[k]))
        if k == 2:
            post.send(swap_u, swap, swap)
        if k > 0:
            phase("halo_wait%d" % (k - 1))
            post.arrive(near[k - 1])
            phase("conv%d" % (k - 1))
            lax.fori_loop((k - 1) * CT // 3, k * CT // 3, conv_tile, 0)
    phase("norm")
    inside = lax.broadcasted_iota(jnp.int32, (W, CP), 1) < C

    def norm_block(r, _):
        at = pl.ds(pl.multiple_of(r * W, W), W)
        v = mx[at, :]
        centered = jnp.where(inside, v - jnp.sum(v, axis=1, keepdims=True) / C, 0.0)
        var = jnp.sum(centered * centered, axis=1, keepdims=True) / C
        inverse = lax.rsqrt(var + NORM_EPSILON)
        n = centered * inverse
        normed[at, :] = n
        inv[at, :] = jnp.broadcast_to(inverse, (W, 128))
        ni[at, :] = (n * prm[1:2, :] + prm[2:3, :]).astype(BF16)
        return 0

    lax.fori_loop(0, R, norm_block, 0)

    three = niall.at[pl.ds(0, 3)]
    ni_copies = post.together(
        [
            remote(ni, niall.at[gy], nsend, nrecv, dev(y=lax.rem(y + i, 4)))
            for i in range(1, 4)
        ],
        remote(three, three, nsend, nrecv, sib),
    )
    niall[gy] = ni[...]

    phase("win_wait")
    stq[...] = jnp.zeros_like(stq)
    stp[...] = jnp.zeros_like(stp)
    red[...] = jnp.zeros_like(red)
    post.moved([win_copy])
    phase("active")

    def active(i, _):
        at = lanes(i, 256)
        bias = [pb_ref[pl.ds(2 * i + k, 1), :] for k in range(2)]
        p = jnp.dot(ni[...], win[:, at], preferred_element_type=F32)
        p = p + jnp.concatenate(bias, axis=1)
        phi = 0.5 * (1.0 + erf(p * HALF_ROOT))
        v = p * phi
        act[:, at] = v
        gp[:, at] = phi + p * (NORMAL_PEAK * jnp.exp(-0.5 * p * p))
        s = jnp.sum(v * v, axis=0, keepdims=True)
        stq[pl.ds(2 * i, 1), :] = s[:, 0:128]
        stq[pl.ds(2 * i + 1, 1), :] = s[:, 128:256]
        return 0

    lax.fori_loop(0, HT // 2, active, 0, unroll=True)

    def to_group(src, dst, send, recv):
        seven = dst.at[pl.ds(0, 7)]
        return post.together(
            [remote(src, dst.at[gx], send, recv, in_gx(i)) for i in range(1, 8)],
            remote(seven, seven, send, recv, sib),
        )

    q_copies = to_group(stq, rq, gsend.at[0], grecv.at[0])
    rq[gx] = stq[...]

    phase("up_wait")
    post.arrive([swap_u])
    post.moved([wout_copy])
    phase("down")
    uf = up[...].reshape(T, CP)

    dg[...] = jnp.dot(uf, wout[...], preferred_element_type=F32)

    def downward(i, _):
        at = lanes(i, 256)
        d = dg[:, at]
        s = jnp.sum(d * act[:, at], axis=0, keepdims=True)
        stp[pl.ds(2 * i, 1), :] = s[:, 0:128]
        stp[pl.ds(2 * i + 1, 1), :] = s[:, 128:256]
        e = jnp.sum(d, axis=0, keepdims=True)
        red[pl.ds(360 + 2 * i, 1), :] = e[:, 0:128]
        red[pl.ds(361 + 2 * i, 1), :] = e[:, 128:256]
        return 0

    lax.fori_loop(0, HT // 2, downward, 0, unroll=True)
    p_copies = to_group(stp, rp, gsend.at[1], grecv.at[1])
    rp[gx] = stp[...]

    phase("response")
    post.arrive(q_copies)
    squares = rq[0, 0:HT]
    for i in range(1, 8):
        squares = squares + rq[i, 0:HT]
    magnitude = jnp.sqrt(squares + RESPONSE_EPSILON)
    denominator = jnp.sum(magnitude) / H + RESPONSE_EPSILON
    response = magnitude / denominator
    coef[0, 0:HT] = 1.0 + rg_ref[...] * response
    red[336 : 336 + HT] = response * stp[0:HT]
    post.arrive(p_copies)
    products = rp[0, 0:HT]
    for i in range(1, 8):
        products = products + rp[i, 0:HT]
    scaled_products = rg_ref[...] * products
    magnitude_grad = scaled_products / denominator - jnp.sum(
        scaled_products * magnitude
    ) / (denominator * denominator * H)
    coef[1, 0:HT] = magnitude_grad / magnitude

    phase("preact")
    own = pl.ds(pl.multiple_of(gy * 128, 128), 128)
    a_copies = [[], []]

    def exchange(h):
        copies = []
        for i in range(1, 8):
            to, m = in_gy(i)
            copies.append(
                remote(pgt.at[h, m], pgr.at[h, :, own], psend.at[h], precv.at[h], to)
            )
        seven = pgt.at[h, pl.ds(0, 7)]
        a_copies[h] = post.together(
            copies, remote(seven, seven, psend.at[h], precv.at[h], sib)
        )

    def backward(h):
        at = pl.ds(h * (H // 2), H // 2)
        return lax.dot_general(
            pg[:, at], win[:, at], (((1,), (1,)), ((), ())), preferred_element_type=F32
        )

    for h in range(2):

        def preact(i, _):
            j = h * (HT // 2) + i
            at = lanes(j)
            a = coef[0, pl.ds(j, 1), :]
            b = coef[1, pl.ds(j, 1), :]
            g = (dg[:, at] * a + act[:, at] * b) * gp[:, at]
            pg[:, at] = g.astype(BF16)
            turned = g.T
            for k in range(16):
                n = i * 16 + k
                q = lax.div(n, B // 8)
                to = (lax.rem(q, 8) * 2 + lax.div(q, 8)) * B + lax.rem(n, B // 8) * 8
                pgtf[pl.ds(pl.multiple_of(to, 8), 8), :] = turned[8 * k : 8 * k + 8, :]
            return 0

        lax.fori_loop(0, HT // 2, preact, 0, unroll=True)
        pgt[h] = pgtf[...].astype(BF16).reshape(8, S // 2, T)
        pgr[h, :, own] = pgt[h, gy]
        if h == 0:
            exchange(0)
            ngb[...] = backward(0)

    phase("normed_grad")
    ngb[...] = ngb[...] + backward(1)
    exchange(1)
    phase("norm_grad")

    def norm_grad(r, sums):
        at = pl.ds(pl.multiple_of(r * W, W), W)
        g = ngb[at, :]
        n = normed[at, :]
        gn = g * n
        s = g * prm[1:2, :]
        m1 = jnp.sum(s, axis=1, keepdims=True) / C
        m2 = jnp.sum(s * n, axis=1, keepdims=True) / C
        v = inv[at, :][:, 0:1] * (s - m1 - n * m2)
        mg[3 + r] = jnp.where(inside, v, 0.0).astype(BF16)
        return (
            sums[0] + jnp.sum(gn, axis=0, keepdims=True),
            sums[1] + jnp.sum(g, axis=0, keepdims=True),
        )

    zero = jnp.zeros((1, CP), F32)
    gain_part, shift_part = lax.fori_loop(0, R, norm_grad, (zero, zero))
    m_copies = halo(mg, 6)

    phase("kernel_grad")
    def kernel_tile(t, _):
        at = lanes(t)
        for i in range(R + 6):
            xf[i] = xs[i, :, at].astype(F32)
        g = [mg[3 + r, :, at].astype(F32) for r in range(R)]
        base = t * 56
        for b in range(7):
            gs = [moved(v, 3 - b) for v in g]
            for a in range(7):
                s = xf[a] * gs[0]
                for r in range(1, R):
                    s = s + xf[a + r] * gs[r]
                red[pl.ds(base + a * 8 + b, 1), :] = jnp.sum(s, axis=0, keepdims=True)
        return 0

    for t in range(CT):
        red[56 * t + 7 : 56 * t + 8, :] = gain_part[:, 128 * t : 128 * t + 128]
        red[56 * t + 15 : 56 * t + 16, :] = shift_part[:, 128 * t : 128 * t + 128]

    def share(m):
        return pl.ds(pl.multiple_of(m * 64, 8), 64)

    adds = gx < 6
    rest = jnp.logical_not(adds)

    def scatter(low, high):
        for i in range(1, 8):
            m = lax.rem(gx + i, 8)
            copy = remote(red.at[share(m)], redr.at[gx], rsend, rrecv, in_gx(i))
            pl.when((m >= low) & (m < high))(copy.start)

    lax.fori_loop(0, 4, kernel_tile, 0)
    scatter(0, 3)
    lax.fori_loop(4, CT, kernel_tile, 0)
    scatter(3, 6)
    sizes = [redr.at[pl.ds(0, k)] for k in (5, 6, 7)]
    five, six, seven = [remote(v, v, rsend, rrecv, sib) for v in sizes]
    r_copies = post.partly([(five, adds), (six, rest)], [(seven, adds)])

    @pl.when(adds)
    def _():
        redr[gx] = red[share(gx), :]

    phase("ni_wait")
    post.arrive(ni_copies)
    pieces = [niall.at[2 * k + core] for k in range(4)]
    four = niall.at[pl.ds(0, 4)]
    f_copies = post.together(
        [remote(p, p, fsend, frecv, sib) for p in pieces],
        remote(four, four, fsend, frecv, sib),
    )

    x_copies = [[], []]

    def weight(h):
        phase("pgr_wait%d" % h)
        post.arrive(a_copies[h])
        if h == 0:
            post.arrive(f_copies)
        phase("dw%d" % h)
        dwf[h, S // 2 :, :] = jnp.zeros((8, CP), F32)
        dwf[h, 0 : S // 2, :] = jnp.dot(
            pgr[h], niall[...].reshape(8 * T, CP), preferred_element_type=F32
        )
        for k in range(4):
            part = jnp.concatenate(
                [dwf[h, B * e + 2 * U * k : B * e + 2 * U * k + 24, :] for e in range(2)]
            )
            dwp[h, k] = part
            dwb[h, k] = part.astype(BF16)
        copies = []
        for i in range(1, 4):
            k = lax.rem(x + i, 4)
            copies.append(
                remote(dwb.at[h, k], xr.at[h, i - 1], xsend.at[h], xrecv.at[h], dev(x=k))
            )
        x_copies[h] = post.together(
            copies, remote(xr.at[h], xr.at[h], xsend.at[h], xrecv.at[h], sib)
        )

    def shares(h):
        phase("x_wait%d" % h)
        post.arrive(x_copies[h])
        phase("z_send%d" % h)
        zacc[h, 48:56, :] = jnp.zeros((8, CP), F32)
        total = dwp[h, x]
        for i in range(3):
            total = total + xr[h, i].astype(F32)
        zacc[h, 0:48, :] = total
        for e in range(2):
            for hi in range(2):
                g = (h * 2 + e) * 2 + hi
                zs[g] = zacc[h, 24 * e + U * hi : 24 * e + U * hi + 16, :].astype(BF16)
                to = hi * 4 + h * 2 + e
                copy = remote(
                    zs.at[g], zr.at[z], zsend, zrecv,
                    dev(zl=jnp.int32(h * 2 + e), zh=jnp.int32(hi)),
                )
                post.together([copy], None, [z != to])
                own_share = pltpu.make_async_copy(zs.at[g], zr.at[z], zlocal)
                pl.when(z == to)(own_share.start)

    weight(0)

    phase("m_wait")
    post.arrive(m_copies)
    phase("back")

    def back_tile(t, _):
        at = lanes(t)
        rows = [mg[i, :, at].astype(F32) for i in range(R + 6)]
        out = depthwise(rows, lambda a, b: ckp[6 - a, 6 - b : 7 - b, at])
        for r in range(R):
            sx[r, :, at] = (out[r] + up[r, :, at].astype(F32)).astype(BF16)
        return 0

    post.left(swap_x)
    o_copies, o_locals = [], []
    for k in range(3):
        lax.fori_loop(k * CT // 3, (k + 1) * CT // 3, back_tile, 0)
        n = min(256, C - 256 * k)
        at = pl.ds(256 * k, n)
        og[:, :, 256 * k : 256 * k + n] = sx[:, :, 256 * k : 256 * k + n]
        src, dst = og.at[:, :, at], ig_ref.at[:, :, at]
        copy = remote(src, dst, osend.at[k], orecv.at[k], swap_dev)
        o_copies.append(post.send(copy, swap, swap))
        copy = pltpu.make_async_copy(src, dst, lsem.at[2 + k])
        o_locals.append(post.move(copy, jnp.logical_not(swap)))

    phase("r_wait")
    post.arrive(r_copies)
    three = remote(yr.at[pl.ds(0, 3)], yr.at[pl.ds(0, 3)], ysend, yrecv, sib)
    y_copies = post.partly([(three, adds)], [(three, adds)])

    @pl.when(adds)
    def _():
        total = redr[0]
        for i in range(1, 8):
            total = total + redr[i]
        ysum[...] = total.reshape(4, 16, 128)
        for i in range(1, 4):
            k = lax.rem(y + i, 4)
            remote(ysum.at[k], yr.at[y], ysend, yrecv, dev(y=k)).start()
        yr[y] = ysum[y]

    weight(1)
    phase("y_wait")
    post.arrive(y_copies)
    seven = remote(zar.at[pl.ds(0, 7)], zar.at[pl.ds(0, 7)], asend, arecv, sib)
    s_copies = post.partly([(seven, adds)], [(seven, adds)])

    @pl.when(adds)
    def _():
        zsum[...] = yr[0] + yr[1] + yr[2] + yr[3]
        for i in range(1, 8):
            remote(zsum, zar.at[z], asend, arecv, in_z(i)).start()
        zar[z] = zsum[...]

    shares(0)
    shares(1)

    phase("s_wait")
    post.arrive(s_copies)
    mine = pl.ds(pl.multiple_of(gx * 64 + y * 16, 8), 16)
    sizes = [red.at[pl.ds(0, 16 * k)] for k in (31, 23, 24)]
    sent, more, all_of = [remote(v, v, qsend, qrecv, sib) for v in sizes]
    l_copies = post.partly([(sent, adds)], [(more, adds), (all_of, rest)])
    own_sums = pltpu.make_async_copy(back, fin.at[mine], lsem.at[1])

    @pl.when(adds)
    def _():
        total = zar[0]
        for i in range(1, 8):
            total = total + zar[i]
        back[...] = total
        for iy, i in layer:
            remote(back, fin.at[mine], qsend, qrecv, in_layer(iy, i)[0]).start()
        own_sums.start()

    post.inside.append((own_sums, adds))
    seven = zs.at[pl.ds(0, 7)]
    z_comes = post.together([], remote(seven, seven, zsend, zrecv, sib))
    phase("z_wait")
    post.arrive(z_comes)
    phase("l_wait")
    post.arrive(l_copies)
    phase("o_wait")
    post.arrive(o_copies)
    post.moved(o_locals + [own_sums])
    pltpu.make_async_copy(zs.at[0], zr.at[z], zlocal).wait()

    phase("sends")
    post.drain()
    phase()


def finish(ig_ref, zr, fin, out_ref, dw_ref, kg_ref, ng_ref, rp_ref):
    out_ref[...] = ig_ref[...]
    scale = 1.0 / math.sqrt(32.0 * 32.0 * 32.0)
    total = zr[0].astype(F32)
    for k in range(1, 8):
        total = total + zr[k].astype(F32)
    dw_ref[...] = total[0:U, 0:C] * scale
    for t in range(CT):
        a0, n = 128 * t, min(128, C - 128 * t)
        for a in range(7):
            row = 56 * t + 8 * a
            kg_ref[a, :, a0 : a0 + n] = fin[row : row + 7, 0:n] * scale
        ng_ref[0:1, a0 : a0 + n] = fin[56 * t + 7 : 56 * t + 8, 0:n] * scale
        ng_ref[1:2, a0 : a0 + n] = fin[56 * t + 15 : 56 * t + 16, 0:n] * scale
    for i in range(HT):
        rp_ref[0:1, 128 * i : 128 * i + 128] = fin[336 + i : 337 + i, :] * scale
        rp_ref[1:2, 128 * i : 128 * i + 128] = fin[360 + i : 361 + i, :] * scale


def shards(
    act_codes, act_exponents, grad_codes, grad_exponents, conv_kernel, conv_bias,
    norm_gain, norm_shift, proj_in, proj_bias, response_gain, proj_out,
):
    vmem = pl.BlockSpec(memory_space=pltpu.VMEM)
    hbm = pl.BlockSpec(memory_space=pl.ANY)
    dma = pltpu.SemaphoreType.DMA
    scratch = [
        pltpu.VMEM((R, W, C), BF16),
        pltpu.VMEM((C // 32, R, W), jnp.int32),
        pltpu.VMEM((R, W, C), BF16),
        pltpu.VMEM((C // 32, R, W), jnp.int32),
        pltpu.VMEM((7, 7, C), F32),
        pltpu.VMEM((C,), F32),
        pltpu.VMEM((C,), F32),
        pltpu.VMEM((C,), F32),
        pltpu.VMEM((HT, 128), F32),
        pltpu.VMEM((HT, 128), F32),
        pltpu.VMEM((CP, H), BF16),
        pltpu.VMEM((CP, H), BF16),
        pltpu.VMEM((7, 8, CP), F32),
        pltpu.VMEM((8, CP), F32),
        pltpu.VMEM((R, W, CP), BF16),
        pltpu.VMEM((R, W, CP), BF16),
        pltpu.VMEM((R + 6, W, CP), BF16),
        pltpu.VMEM((R, W, CP), BF16),
        pltpu.VMEM((R + 6, W, CP), BF16),
        pltpu.VMEM((T, CP), F32),
        pltpu.VMEM((T, CP), F32),
        pltpu.VMEM((T, 128), F32),
        pltpu.VMEM((T, CP), BF16),
        pltpu.VMEM((8, T, CP), BF16),
        pltpu.VMEM((T, H), F32),
        pltpu.VMEM((T, H), F32),
        pltpu.VMEM((T, H), F32),
        pltpu.VMEM((T, H), BF16),
        pltpu.VMEM((H // 2, T), F32),
        pltpu.VMEM((2, 8, S // 2, T), BF16),
        pltpu.VMEM((2, S // 2, 8 * T), BF16),
        pltpu.VMEM((24, 128), F32),
        pltpu.VMEM((24, 128), F32),
        pltpu.VMEM((8, 24, 128), F32),
        pltpu.VMEM((8, 24, 128), F32),
        pltpu.VMEM((2, 24, 128), F32),
        pltpu.VMEM((2, S // 2 + 8, CP), F32),
        pltpu.VMEM((2, 4, 48, CP), F32),
        pltpu.VMEM((2, 4, 48, CP), BF16),
        pltpu.VMEM((2, 3, 48, CP), BF16),
        pltpu.VMEM((2, 56, CP), F32),
        pltpu.VMEM((8, 16, CP), BF16),
        pltpu.VMEM((T, CP), F32),
        pltpu.VMEM((R + 6, W, 128), F32),
        pltpu.VMEM((512, 128), F32),
        pltpu.VMEM((8, 64, 128), F32),
        pltpu.VMEM((4, 16, 128), F32),
        pltpu.VMEM((4, 16, 128), F32),
        pltpu.VMEM((16, 128), F32),
        pltpu.VMEM((8, 16, 128), F32),
        pltpu.VMEM((16, 128), F32),
        pltpu.VMEM((R, W, C), BF16),
        dma((2,)), dma((10,)),
        dma((4,)), dma((4,)),
        dma((8,)), dma((8,)),
        dma((2,)), dma((2,)),
        dma, dma,
        dma, dma,
        dma((2,)), dma((2,)),
        dma((5,)),
        dma((2,)), dma((2,)),
        dma, dma,
        dma, dma,
        dma, dma,
        dma,
        dma, dma,
        dma, dma,
        dma((3,)), dma((3,)),
    ]
    outs = pl.pallas_call(
        body,
        out_shape=(
            jax.ShapeDtypeStruct((R, W, C), BF16),
            jax.ShapeDtypeStruct((8, 16, CP), BF16),
            jax.ShapeDtypeStruct((512, 128), F32),
        ),
        in_specs=[hbm] * 12,
        out_specs=(hbm,) * 3,
        scratch_shapes=scratch,
        compiler_params=pltpu.CompilerParams(
            collective_id=0, has_side_effects=True, vmem_limit_bytes=56 * 1024 * 1024
        ),
    )(
        act_codes[0],
        act_exponents[0].transpose(2, 0, 1),
        grad_codes[0],
        grad_exponents[0].transpose(2, 0, 1),
        conv_kernel,
        conv_bias,
        norm_gain,
        norm_shift,
        proj_in.T,
        proj_bias.reshape(HT, 128),
        response_gain.reshape(HT, 128),
        proj_out.T,
    )
    results = pl.pallas_call(
        finish,
        out_shape=(
            jax.ShapeDtypeStruct((R, W, C), BF16),
            jax.ShapeDtypeStruct((U, C), F32),
            jax.ShapeDtypeStruct((7, 7, C), F32),
            jax.ShapeDtypeStruct((2, C), F32),
            jax.ShapeDtypeStruct((2, H), F32),
        ),
        in_specs=[vmem] * 3,
        out_specs=(vmem,) * 5,
    )(*outs)
    return (results[0][None],) + tuple(results[1:])


def solution(mesh):
    strips = P("dp", "rows", None, None)
    return jax.shard_map(
        shards,
        mesh=mesh,
        in_specs=(strips,) * 4 + (P(),) * 8,
        out_specs=(strips, P(("dp", "rows"), None), P(), P(), P()),
        check_vma=False,
    )
```
